256 devices in a mesh: dp: 8 (over x, core), seq: 32 (over z, y).
Axes of the slice: x: 4, y: 4, z: 8, core: 2. Of those that a mesh axis runs over, the one named last changes fastest.
Arguments:
- frames: bfloat16 [8, 4096, 1024], P('dp', 'seq'), may hold values from -6 to 6
- segment_ids: int32 [8, 4096], P('dp', 'seq'), may hold values from 0 to 15, never falling along the last dimension, each value on 1 to 768 neighbouring positions
- norm_gain: float32 [1024], replicated, may hold values from 0.1 to 1.9
- w_qkv: bfloat16 [1024, 3072], replicated, as said below
- w_out: bfloat16 [1024, 1024], replicated, may hold values from -0.1875 to 0.1875
- cotangent: bfloat16 [8, 4096, 1024], P('dp', 'seq'), may hold values from -6 to 6
Outputs:
- block_out: bfloat16 [8, 4096, 1024], P('dp', 'seq')
- out_grad: float32 [1024, 1024], P('seq', 'dp')
The draws below stay inside these ranges and needn't reach their ends.
Inputs may be any that keep to these rules, and one draw needn't show every extreme that they name: `segment_ids`: within each data group, utterance numbers never fall along the frames; each utterance covers 1 to 768 frames, and some utterance covers exactly 768. `w_qkv`: projection weights of magnitude below 1; query-key products of some heads can be large.
All inputs are finite; a program needn't handle non-finite values.
Results may differ from the reference program's by a relative error of at most 0.025.
Values may be sent and summed in bfloat16 or wider, within the bound.
No kernel may reach another device: no remote copies, remote signals or barrier semaphores. Data moves between devices by JAX's collectives and lax.ppermute only.
A program may use at most 128 MiB of HBM per device.

```python
import math
import jax
import jax.numpy as jnp
import numpy as np
from jax import lax

D = 1024
HEADS = 16
HEAD_DIM = 64
FR = 128
SPAN = 6
GF = 4096
MOST = 768
UTTS = 16
N_DP = 8
N_SEQ = 32


def draw_w_qkv(key, part):
    key = jax.random.fold_in(key, 11)
    normal_entries = jax.random.normal(key, (D, 3 * D), jnp.float32) * D ** (-0.5)
    return normal_entries.astype(jnp.bfloat16)


def strengthened(result, stream_key, source, target, blocks, factor):
    def block_of(dim):
        return (jnp.arange(result.shape[dim]) // (result.shape[dim] // blocks)).reshape((-1,) + (1,) * (result.ndim - 1 - dim))

    one_side = jax.random.permutation(stream_key, blocks)[block_of(target)]
    other_side = (block_of(target) + blocks // 2) % blocks
    return jnp.where((block_of(source) == one_side) | (block_of(source) == other_side), factor * result, result)


def block_scale(stream_key, dims, shards, low, high):
    level = 1.0
    for axis_at, parts in shards:
        steps = jax.random.uniform(jax.random.fold_in(jax.random.fold_in(stream_key, 6), axis_at), (parts,), jnp.float32, low / len(shards), high / len(shards))
        level = level * jnp.repeat(jnp.exp(steps), dims[axis_at] // parts).reshape((-1,) + (1,) * (len(dims) - 1 - axis_at))
    return level


def length_profile(amount, total, reach, slope):
    loads = [(1 << 20) // math.isqrt(rank ** slope) + 1 for rank in range(2, amount + 1)]
    surplus, holding = total - reach - (amount - 1), [1] * (amount - 1)
    while surplus > 0:
        movable = [i for i in range(amount - 1) if holding[i] < reach]
        pool, remaining = sum([loads[i] for i in movable]), surplus
        for i in movable:
            more = min(reach - holding[i], max(1, remaining * loads[i] // pool), surplus)
            holding[i] = holding[i] + more
            surplus = surplus - more
    return np.array([reach] + holding)


def uneven(stream_key, count, total, reach, lean):
    if count == 2:
        one = jax.random.randint(stream_key, (), max(1, total - reach), min(reach, total - 1) + 1)
        return jnp.stack([one, total - one])
    lengths = jnp.asarray(length_profile(count, total, reach, lean), jnp.int32)
    pairs = (count - 1) // 2
    source_of, taker = lengths[1:1 + 2 * pairs:2], lengths[2:2 + 2 * pairs:2]
    room = jnp.minimum(source_of - 1, reach - taker)
    shifted = jax.random.randint(jax.random.fold_in(stream_key, 1), (pairs,), 0, 1 << 20) % (room + 1)
    lengths = lengths.at[1:1 + 2 * pairs:2].set(source_of - shifted).at[2:2 + 2 * pairs:2].set(taker + shifted)
    return lengths[jax.random.permutation(jax.random.fold_in(stream_key, 2), count)]


def scatter_about(stream_key, shape, scale, most, shards=(), held_as=jnp.bfloat16):
    entries = jax.random.normal(stream_key, shape, jnp.float32) * scale
    if len(shards) > 0:
        entries = block_scale(stream_key, shape, shards, -0.22, 0.18) * entries
    return jnp.clip(entries, min=-most, max=most).astype(held_as)


def bell_draw_with(own_key, dims, width, most, shards, heavy, held_as=jnp.bfloat16):
    drawn = width * jax.random.normal(own_key, dims, jnp.float32)
    if shards:
        drawn = drawn * block_scale(own_key, dims, shards, -0.22, 0.18)
    return jnp.clip(strengthened(drawn, jax.random.fold_in(own_key, 3), *heavy), -most, most).astype(held_as)


def setup_inputs(seed: int = 0) -> dict:
    key_of = jax.random.split(jax.random.key(seed), 7)
    return {
        "frames": scatter_about(key_of[0], (N_DP, GF, D), 1.0, 6.0, ((0, 8), (1, 32))),
        "segment_ids": jax.vmap(lambda own: jnp.searchsorted(jnp.cumsum(uneven(own, UTTS, GF, MOST, 2)), jnp.arange(GF), side="right"))(jax.random.split(key_of[1], N_DP)).reshape((N_DP, GF)).astype(jnp.int32),
        "norm_gain": jnp.clip(1.0 + 0.18 * jax.random.normal(key_of[2], (D,), jnp.float32), 0.1, 1.9),
        "w_qkv": draw_w_qkv(jax.random.fold_in(key_of[6], 71), 0),
        "w_out": scatter_about(key_of[4], (D, D), D ** -0.5, 0.1875),
        "cotangent": bell_draw_with(key_of[5], (N_DP, GF, D), 1.0, 6.0, ((0, 8), (1, 32)), (1, 2, 32, 2.75)),
    }


NEG_BIG = -1e+30
EPSILON = 1e-05

def normalize(frames_block, norm_gain):
    float_frames = frames_block.astype(jnp.float32)
    average = lax.optimization_barrier(jnp.mean(float_frames, axis=-1, keepdims=True))
    centered = float_frames - average
    variance = lax.optimization_barrier(jnp.mean(centered * centered, axis=-1, keepdims=True))
    return (centered * lax.rsqrt(variance + EPSILON) * norm_gain).astype(jnp.bfloat16)

def reference(frames, segment_ids, norm_gain, w_qkv, w_out, cotangent):
    margin_rows = SPAN * FR
    window = (2 * SPAN + 1) * FR
    score_scale = HEAD_DIM ** (-0.5)
    grad_scale = (N_DP * GF) ** (-0.5)

    def one_group(grad_sum, group_args):
        group_frames, group_ids, group_grads = group_args
        normed = normalize(group_frames, norm_gain)
        projected = jnp.dot(normed, w_qkv, preferred_element_type=jnp.float32).astype(jnp.bfloat16)
        queries = projected[:, :D].reshape(GF, HEADS, HEAD_DIM)
        keys_all = jnp.pad(projected[:, D:2 * D].reshape(GF, HEADS, HEAD_DIM), ((margin_rows, margin_rows), (0, 0), (0, 0)))
        values_all = jnp.pad(projected[:, 2 * D:].reshape(GF, HEADS, HEAD_DIM), ((margin_rows, margin_rows), (0, 0), (0, 0)))
        utter_ids = group_ids + 1
        padded_ids = jnp.pad(utter_ids, (margin_rows, margin_rows))

        def one_block(block_index):
            first_row = (block_index * FR).astype(jnp.int32)
            block_queries = lax.dynamic_slice_in_dim(queries, first_row, FR, 0).astype(jnp.float32)
            block_ids = lax.dynamic_slice_in_dim(utter_ids, first_row, FR, 0)
            near_keys = lax.dynamic_slice_in_dim(keys_all, first_row, window, 0).astype(jnp.float32)
            near_values = lax.dynamic_slice_in_dim(values_all, first_row, window, 0).astype(jnp.float32)
            near_ids = lax.dynamic_slice_in_dim(padded_ids, first_row, window, 0)
            scores = jnp.einsum('qhd,khd->qhk', block_queries, near_keys) * score_scale
            same_utterance = (block_ids[:, None] == near_ids[None, :])[:, None, :]
            scores = jnp.where(same_utterance, scores, NEG_BIG)
            row_top = lax.optimization_barrier(jnp.max(scores, axis=-1, keepdims=True))
            attn_weights = jnp.where(same_utterance, jnp.exp(scores - row_top), 0.0)
            row_total = lax.optimization_barrier(jnp.sum(attn_weights, axis=-1))
            rounded = lax.optimization_barrier(attn_weights.astype(jnp.bfloat16)).astype(jnp.float32)
            mixed = jnp.einsum('qhk,khd->qhd', rounded, near_values)
            return (mixed / row_total[..., None]).reshape(FR, D)
        attended = lax.map(one_block, jnp.arange(N_SEQ, dtype=jnp.int32)).reshape(GF, D).astype(jnp.bfloat16)
        group_out = (group_frames.astype(jnp.float32) + jnp.dot(attended, w_out, preferred_element_type=jnp.float32)).astype(jnp.bfloat16)
        grad_term = lax.dot_general(attended, group_grads, (((0,), (0,)), ((), ())), preferred_element_type=jnp.float32)
        return (grad_sum + grad_term, group_out)
    grad_sum, block_out = lax.scan(one_group, jnp.zeros((D, D), jnp.float32), (frames, segment_ids, cotangent))
    return (block_out, grad_sum * grad_scale)
```

```python
import functools

import jax
import jax.numpy as jnp
from jax import lax
from jax.experimental import pallas as pl
from jax.experimental.pallas import tpu as pltpu
from jax.sharding import PartitionSpec as P

HEADS = 16
ROWS = 128
LANES = 128
WIDTH = 1024
CHUNKS = WIDTH // LANES
PACKED = WIDTH + 16
QUAD = 256
QUADS = WIDTH // QUAD
NEG_BIG = -1e30
EPSILON = 1e-05
LOG2E = 1.4426950408889634
F32 = jnp.float32
BF16 = jnp.bfloat16


def vmem_limit(mib):
    return pltpu.CompilerParams(vmem_limit_bytes=mib * 1024 * 1024)


def shifted(block, distance):
    devices = range(lax.axis_size("seq"))
    route = [(i - distance, i) for i in devices if i - distance in devices]
    return lax.ppermute(block, "seq", route)


def norm_kernel(frames_ref, ids_ref, gain_ref, packed_ref):
    float_frames = frames_ref[...].astype(F32)
    average = jnp.mean(float_frames, axis=-1, keepdims=True)
    centered = float_frames - average
    variance = jnp.mean(centered * centered, axis=-1, keepdims=True)
    normed = (centered * lax.rsqrt(variance + EPSILON) * gain_ref[...]).astype(BF16)
    for c in range(CHUNKS):
        packed_ref[c * ROWS : (c + 1) * ROWS, :] = normed[:, c * LANES : (c + 1) * LANES]
    ids = (ids_ref[...] + 1).astype(F32)
    packed_ref[WIDTH:PACKED, :] = jnp.broadcast_to(ids, (16, LANES)).astype(BF16)


def normalize(frames, ids, gain):
    return pl.pallas_call(
        norm_kernel,
        out_shape=jax.ShapeDtypeStruct((PACKED, LANES), BF16),
        name="layer_norm",
    )(frames, ids, gain)


def unpacked(ref):
    return jnp.concatenate([ref[c * ROWS : (c + 1) * ROWS, :] for c in range(CHUNKS)], axis=1)


def id_row(ref):
    return ref[WIDTH:PACKED, :].astype(F32)[0:1, :]


def id_column(row):
    across = lax.broadcasted_iota(jnp.int32, (ROWS, LANES), 1)
    down = lax.broadcasted_iota(jnp.int32, (ROWS, LANES), 0)
    return jnp.sum(jnp.where(across == down, row, 0.0), axis=1, keepdims=True)


def low_half():
    return lax.broadcasted_iota(jnp.int32, (ROWS, LANES), 1) < LANES // 2


def pair_queries(queries):
    low = low_half()
    zeros = jnp.zeros_like(queries)
    return jnp.concatenate([jnp.where(low, queries, zeros), jnp.where(low, zeros, queries)], axis=0)


def pair_scores(queries, keys, mask):
    scores = lax.dot_general(
        pair_queries(queries), keys, (((1,), (1,)), ((), ())), preferred_element_type=F32
    )
    return jnp.where(jnp.concatenate([mask, mask], axis=0), scores * LOG2E, NEG_BIG)


def side_by_side(stacked):
    return jnp.where(low_half(), stacked[:ROWS], stacked[ROWS:])


def column(block, index):
    return block[:, index : index + 1]


def with_columns(block, columns):
    lane = lax.broadcasted_iota(jnp.int32, (ROWS, LANES), 1)
    for index, values in columns:
        block = jnp.where(lane == index, values, block)
    return block


def first_absorb(queries, keys, values, mask, tops_ref, sums_ref, acc_ref):
    tops = jnp.zeros((ROWS, LANES), F32)
    sums = jnp.zeros((ROWS, LANES), F32)
    for pair in range(2):
        at = slice(pair * LANES, (pair + 1) * LANES)
        scores = pair_scores(queries[:, at], keys[:, at], mask)
        top = jnp.max(scores, axis=1, keepdims=True)
        weights = jnp.exp2(scores - top)
        total = jnp.sum(weights, axis=1, keepdims=True)
        mixed = jnp.dot(weights.astype(BF16), values[:, at], preferred_element_type=F32)
        tops = with_columns(tops, ((2 * pair, top[:ROWS]), (2 * pair + 1, top[ROWS:])))
        sums = with_columns(sums, ((2 * pair, total[:ROWS]), (2 * pair + 1, total[ROWS:])))
        acc_ref[:, at] = side_by_side(mixed)
    tops_ref[...] = tops
    sums_ref[...] = sums


def next_absorb(queries, keys, values, mask, tops_ref, sums_ref, acc_ref):
    tops = tops_ref[...]
    sums = sums_ref[...]
    for pair in range(2):
        at = slice(pair * LANES, (pair + 1) * LANES)
        one, two = 2 * pair, 2 * pair + 1
        scores = pair_scores(queries[:, at], keys[:, at], mask)
        old_top = jnp.concatenate([column(tops, one), column(tops, two)], axis=0)
        old_sum = jnp.concatenate([column(sums, one), column(sums, two)], axis=0)
        top = jnp.maximum(old_top, jnp.max(scores, axis=1, keepdims=True))
        rescale = jnp.exp2(old_top - top)
        weights = jnp.exp2(scores - top)
        total = old_sum * rescale + jnp.sum(weights, axis=1, keepdims=True)
        mixed = jnp.dot(weights.astype(BF16), values[:, at], preferred_element_type=F32)
        tops = with_columns(tops, ((one, top[:ROWS]), (two, top[ROWS:])))
        sums = with_columns(sums, ((one, total[:ROWS]), (two, total[ROWS:])))
        scale = jnp.where(low_half(), rescale[:ROWS], rescale[ROWS:])
        acc_ref[:, at] = acc_ref[:, at] * scale + side_by_side(mixed)
    tops_ref[...] = tops
    sums_ref[...] = sums


def projected(frames, weight_ref):
    return jnp.dot(frames, weight_ref[...], preferred_element_type=F32).astype(BF16)


def own_kernel(own_ref, wq_ref, wk_ref, wv_ref, queries_ref, tops_ref, sums_ref, acc_ref):
    frames = unpacked(own_ref)
    row = id_row(own_ref)
    mask = id_column(row) == row
    queries = projected(frames, wq_ref) * jnp.asarray(0.125, BF16)
    queries_ref[...] = queries
    keys = projected(frames, wk_ref)
    values = projected(frames, wv_ref)
    first_absorb(queries, keys, values, mask, tops_ref, sums_ref, acc_ref)


def weight_spec(section):
    return pl.BlockSpec((WIDTH, QUAD), lambda j: (0, section * QUADS + j))


PACKED_SPEC = pl.BlockSpec((PACKED, LANES), lambda j: (0, 0))
COLUMN_SPEC = pl.BlockSpec((ROWS, QUAD), lambda j: (0, j))
STAT_SPEC = pl.BlockSpec((None, ROWS, LANES), lambda j: (j, 0, 0))
STATE_SHAPES = (
    jax.ShapeDtypeStruct((QUADS, ROWS, LANES), F32),
    jax.ShapeDtypeStruct((QUADS, ROWS, LANES), F32),
    jax.ShapeDtypeStruct((ROWS, WIDTH), F32),
)


def own_block(own, w_qkv):
    return pl.pallas_call(
        own_kernel,
        grid=(QUADS,),
        in_specs=[PACKED_SPEC, weight_spec(0), weight_spec(1), weight_spec(2)],
        out_specs=[COLUMN_SPEC, STAT_SPEC, STAT_SPEC, COLUMN_SPEC],
        out_shape=[jax.ShapeDtypeStruct((ROWS, WIDTH), BF16), *STATE_SHAPES],
        compiler_params=vmem_limit(24),
        cost_estimate=pl.CostEstimate(
            flops=2 * ROWS * WIDTH * 3 * WIDTH, bytes_accessed=7 << 20, transcendentals=0
        ),
        name="own_block",
    )(own, w_qkv, w_qkv, w_qkv)


def absorb_group(near_ref, far_ref, own_row, queries, wk_ref, wv_ref, state):
    frames = jnp.concatenate([unpacked(near_ref), unpacked(far_ref)], axis=0)
    keys = projected(frames, wk_ref)
    values = projected(frames, wv_ref)
    rows = jnp.concatenate([id_row(near_ref), id_row(far_ref)], axis=1)
    mask = id_column(own_row) == rows
    next_absorb(queries, keys, values, mask, *state)


def absorb_both(own_ref, left_near, left_far, right_near, right_far, queries_ref, wk_ref, wv_ref, state):
    own_row = id_row(own_ref)
    left_needed = jnp.max(id_row(left_near)) == jnp.min(own_row)
    right_needed = jnp.min(id_row(right_near)) == jnp.max(own_row)

    @pl.when(left_needed)
    def _():
        absorb_group(left_near, left_far, own_row, queries_ref[...], wk_ref, wv_ref, state)

    @pl.when(right_needed)
    def _():
        absorb_group(right_near, right_far, own_row, queries_ref[...], wk_ref, wv_ref, state)


def stage_kernel(
    own_ref, left_near, left_far, right_near, right_far, queries_ref, wk_ref, wv_ref,
    old_tops, old_sums, old_acc, tops_ref, sums_ref, acc_ref,
):
    tops_ref[...] = old_tops[...]
    sums_ref[...] = old_sums[...]
    acc_ref[...] = old_acc[...]
    state = (tops_ref, sums_ref, acc_ref)
    absorb_both(own_ref, left_near, left_far, right_near, right_far, queries_ref, wk_ref, wv_ref, state)


STAGE_COST = pl.CostEstimate(
    flops=2 * 4 * ROWS * WIDTH * 2 * WIDTH, bytes_accessed=8 << 20, transcendentals=0
)


def absorb_stage(own, near_far, queries, w_qkv, state):
    return pl.pallas_call(
        stage_kernel,
        grid=(QUADS,),
        in_specs=[PACKED_SPEC] * 5
        + [COLUMN_SPEC, weight_spec(1), weight_spec(2), STAT_SPEC, STAT_SPEC, COLUMN_SPEC],
        out_specs=[STAT_SPEC, STAT_SPEC, COLUMN_SPEC],
        out_shape=list(STATE_SHAPES),
        compiler_params=vmem_limit(32),
        cost_estimate=STAGE_COST,
        name="absorb_stage",
    )(own, *near_far, queries, w_qkv, w_qkv, *state)


def last_kernel(
    own_ref, left_near, left_far, right_near, right_far, queries_ref, wk_ref, wv_ref,
    old_tops, old_sums, old_acc, frames_ref, wout_ref, attended_ref, out_ref,
    tops_ref, sums_ref, acc_ref, total_ref,
):
    quad = pl.program_id(0)
    tops_ref[...] = old_tops[...]
    sums_ref[...] = old_sums[...]
    acc_ref[...] = old_acc[...]
    state = (tops_ref, sums_ref, acc_ref)
    absorb_both(own_ref, left_near, left_far, right_near, right_far, queries_ref, wk_ref, wv_ref, state)
    sums = sums_ref[...]
    parts = []
    for pair in range(2):
        at = slice(pair * LANES, (pair + 1) * LANES)
        divisor = jnp.where(low_half(), column(sums, 2 * pair), column(sums, 2 * pair + 1))
        part = (acc_ref[:, at] / divisor).astype(BF16)
        attended_ref[pair] = part
        parts.append(part)
    term = jnp.dot(jnp.concatenate(parts, axis=1), wout_ref[...], preferred_element_type=F32)

    @pl.when(quad == 0)
    def _():
        total_ref[...] = frames_ref[...].astype(F32) + term

    @pl.when(quad > 0)
    def _():
        total_ref[...] += term

    @pl.when(quad == QUADS - 1)
    def _():
        out_ref[...] = total_ref[...].astype(BF16)


def last_stage(own, near_far, queries, w_qkv, state, frames, w_out):
    return pl.pallas_call(
        last_kernel,
        grid=(QUADS,),
        in_specs=[PACKED_SPEC] * 5
        + [COLUMN_SPEC, weight_spec(1), weight_spec(2), STAT_SPEC, STAT_SPEC, COLUMN_SPEC]
        + [
            pl.BlockSpec((ROWS, WIDTH), lambda j: (0, 0)),
            pl.BlockSpec((QUAD, WIDTH), lambda j: (j, 0)),
        ],
        out_specs=[
            pl.BlockSpec((2, ROWS, LANES), lambda j: (j, 0, 0)),
            pl.BlockSpec((ROWS, WIDTH), lambda j: (0, 0)),
        ],
        out_shape=[
            jax.ShapeDtypeStruct((CHUNKS, ROWS, LANES), BF16),
            jax.ShapeDtypeStruct((ROWS, WIDTH), BF16),
        ],
        scratch_shapes=[
            pltpu.VMEM((ROWS, LANES), F32),
            pltpu.VMEM((ROWS, LANES), F32),
            pltpu.VMEM((ROWS, QUAD), F32),
            pltpu.VMEM((ROWS, WIDTH), F32),
        ],
        compiler_params=vmem_limit(32),
        cost_estimate=STAGE_COST,
        name="last_stage",
    )(own, *near_far, queries, w_qkv, w_qkv, *state, frames, w_out)


def grad_kernel(attended_ref, cotangent_ref, out_ref):
    product = lax.dot_general(
        attended_ref[...], cotangent_ref[...], (((0,), (0,)), ((), ())), preferred_element_type=F32
    ).astype(BF16)
    for half in range(2):
        out_ref[half] = product[:, half * LANES : (half + 1) * LANES]


def grad_product(attended, cotangent):
    frames = attended.shape[0]
    return pl.pallas_call(
        grad_kernel,
        grid=(QUADS,),
        in_specs=[
            pl.BlockSpec((frames, LANES), lambda j: (0, 0)),
            pl.BlockSpec((frames, QUAD), lambda j: (0, j)),
        ],
        out_specs=pl.BlockSpec((2, LANES, LANES), lambda j: (j, 0, 0)),
        out_shape=jax.ShapeDtypeStruct((CHUNKS, LANES, LANES), BF16),
        compiler_params=vmem_limit(16),
        name="grad_product",
    )(attended, cotangent)


def local(frames, segment_ids, norm_gain, w_qkv, w_out, cotangent):
    n_dp = lax.axis_size("dp")
    n_seq = lax.axis_size("seq")
    frames = frames[0]
    own = normalize(frames, segment_ids, norm_gain[None, :])
    all_grads = lax.all_gather(cotangent[0], "dp", axis=0, tiled=True)

    left1, right1 = shifted(own, 1), shifted(own, -1)
    left4, right4 = shifted(own, 4), shifted(own, -4)
    queries, *state = own_block(own, w_qkv)

    left2, right2 = shifted(left1, 1), shifted(right1, -1)
    left5, right5 = shifted(left1, 4), shifted(right1, -4)
    state = absorb_stage(own, (left1, left4, right1, right4), queries, w_qkv, state)

    left3, right3 = shifted(left2, 1), shifted(right2, -1)
    left6, right6 = shifted(left2, 4), shifted(right2, -4)
    state = absorb_stage(own, (left2, left5, right2, right5), queries, w_qkv, state)

    attended, block_out = last_stage(
        own, (left3, left6, right3, right6), queries, w_qkv, state, frames, w_out
    )

    swapped = lax.all_to_all(attended, "dp", 0, 0, tiled=True)
    share = grad_product(swapped.reshape(n_dp * ROWS, LANES), all_grads)
    pieces = lax.all_to_all(share.reshape(n_seq, LANES * CHUNKS // n_seq, LANES), "seq", 0, 0, tiled=True)
    grad_scale = (n_dp * n_seq * ROWS) ** (-0.5)
    block = jnp.sum(pieces.astype(F32), axis=0) * grad_scale
    inner = n_seq // n_dp
    route = [
        (p * n_seq + q * inner + r, q * n_seq + p * inner + r)
        for p in range(n_dp)
        for q in range(n_dp)
        for r in range(inner)
    ]
    return (block_out[None], lax.ppermute(block, ("dp", "seq"), route))


def solution(mesh):
    placed = (P("dp", "seq", None), P("dp", "seq"), P(), P(), P(), P("dp", "seq", None))
    return jax.shard_map(
        local,
        mesh=mesh,
        in_specs=placed,
        out_specs=(P("dp", "seq", None), P("seq", "dp")),
        check_vma=False,
    )
```

```python
import jax
import jax.numpy as jnp
from jax import lax
from jax.experimental import pallas as pl
from jax.experimental.pallas import tpu as pltpu
from jax.sharding import PartitionSpec as P

ROWS = 128
LANES = 128
HALF = 64
WIDTH = 1024
CHUNKS = WIDTH // LANES
PACKED = WIDTH + 16
QUAD = 256
QUADS = WIDTH // QUAD
NEG_BIG = -1e30
EPSILON = 1e-05
LOG2E = 1.4426950408889634
F32 = jnp.float32
BF16 = jnp.bfloat16
LIMIT = pltpu.CompilerParams(vmem_limit_bytes=24 * 1024 * 1024)


def shifted(block, distance):
    n_seq = lax.axis_size("seq")
    route = [(i, (i + distance) % n_seq) for i in range(n_seq)]
    return lax.ppermute(block, "seq", route)


def norm_kernel(frames_ref, ids_ref, gain_ref, packed_ref):
    float_frames = frames_ref[...].astype(F32)
    average = jnp.mean(float_frames, axis=-1, keepdims=True)
    centered = float_frames - average
    variance = jnp.mean(centered * centered, axis=-1, keepdims=True)
    normed = (centered * lax.rsqrt(variance + EPSILON) * gain_ref[...]).astype(BF16)
    for c in range(CHUNKS):
        packed_ref[c * ROWS : (c + 1) * ROWS, :] = normed[:, c * LANES : (c + 1) * LANES]
    ids = (ids_ref[...] + 1).astype(F32)
    packed_ref[WIDTH:PACKED, :] = jnp.broadcast_to(ids, (16, LANES)).astype(BF16)


def normalize(frames, ids, gain):
    return pl.pallas_call(
        norm_kernel,
        out_shape=jax.ShapeDtypeStruct((PACKED, LANES), BF16),
        compiler_params=LIMIT,
        name="layer_norm",
    )(frames, ids, gain)


def unpacked(block):
    ref, slot = block
    base = slot * PACKED
    chunks = [ref[base + c * ROWS : base + (c + 1) * ROWS, :] for c in range(CHUNKS)]
    return jnp.concatenate(chunks, axis=1)


def id_row(block):
    ref, slot = block
    base = slot * PACKED + WIDTH
    return ref[base : base + 16, :].astype(F32)[0:1, :]


def id_column(row):
    across = lax.broadcasted_iota(jnp.int32, (ROWS, LANES), 1)
    down = lax.broadcasted_iota(jnp.int32, (ROWS, LANES), 0)
    return jnp.sum(jnp.where(across == down, row, 0.0), axis=1, keepdims=True)


def projected(frames, weight_ref):
    return jnp.dot(frames, weight_ref[...], preferred_element_type=F32).astype(BF16)


def absorb(queries_ref, keys, values, mask, tops_ref, sums_ref, acc_ref, first):
    flipped = jnp.transpose(values)
    both = jnp.concatenate([mask, mask], axis=1)
    for pair in range(2):
        at = slice(pair * LANES, (pair + 1) * LANES)
        heads = (2 * pair, 2 * pair + 1)
        scores = lax.dot_general(
            keys[:, at], queries_ref[pair], (((1,), (1,)), ((), ())), preferred_element_type=F32
        )
        scores = jnp.where(both, scores * LOG2E, NEG_BIG)
        top = jnp.max(scores, axis=0, keepdims=True)
        if not first:
            old_top = jnp.concatenate([tops_ref[h : h + 1, :] for h in heads], axis=1)
            old_sum = jnp.concatenate([sums_ref[h : h + 1, :] for h in heads], axis=1)
            top = jnp.maximum(old_top, top)
            rescale = jnp.exp2(old_top - top)
        weights = jnp.exp2(scores - top)
        total = jnp.sum(weights, axis=0, keepdims=True)
        mixed = jnp.dot(flipped[at, :], weights.astype(BF16), preferred_element_type=F32)
        if not first:
            total = old_sum * rescale + total
        for k, h in enumerate(heads):
            lanes = slice(k * LANES, (k + 1) * LANES)
            rows = slice(h * HALF, (h + 1) * HALF)
            term = mixed[k * HALF : (k + 1) * HALF, lanes]
            if not first:
                term = acc_ref[rows, :] * rescale[:, lanes] + term
            acc_ref[rows, :] = term
            tops_ref[h : h + 1, :] = top[:, lanes]
            sums_ref[h : h + 1, :] = total[:, lanes]


def own_kernel(own_ref, wq_ref, wk_ref, wv_ref, queries_ref, tops_ref, sums_ref, acc_ref):
    frames = unpacked((own_ref, 0))
    row = id_row((own_ref, 0))
    queries = projected(frames, wq_ref) * jnp.asarray(0.125, BF16)
    low = lax.broadcasted_iota(jnp.int32, (ROWS, LANES), 1) < HALF
    for pair in range(2):
        block = queries[:, pair * LANES : (pair + 1) * LANES]
        zeros = jnp.zeros_like(block)
        queries_ref[pair, 0:ROWS, :] = jnp.where(low, block, zeros)
        queries_ref[pair, ROWS:, :] = jnp.where(low, zeros, block)
    keys = projected(frames, wk_ref)
    values = projected(frames, wv_ref)
    absorb(queries_ref, keys, values, id_column(row) == row, tops_ref, sums_ref, acc_ref, True)


def weight_spec(section):
    return pl.BlockSpec((WIDTH, QUAD), lambda j: (0, section * QUADS + j))


def packed_spec(block):
    return pl.BlockSpec(block.shape, lambda j: (0, 0))


QUERY_SPEC = pl.BlockSpec((2, 2 * ROWS, LANES), lambda j: (j, 0, 0))
STATE_SPECS = (
    pl.BlockSpec((None, 8, LANES), lambda j: (j, 0, 0)),
    pl.BlockSpec((None, 8, LANES), lambda j: (j, 0, 0)),
    pl.BlockSpec((QUAD, LANES), lambda j: (j, 0)),
)
STATE_SHAPES = (
    jax.ShapeDtypeStruct((QUADS, 8, LANES), F32),
    jax.ShapeDtypeStruct((QUADS, 8, LANES), F32),
    jax.ShapeDtypeStruct((WIDTH, LANES), F32),
)


def cost(blocks, mib):
    return pl.CostEstimate(
        flops=2 * blocks * ROWS * WIDTH * 2 * WIDTH, bytes_accessed=mib << 20, transcendentals=0
    )


def own_block(own, w_qkv):
    return pl.pallas_call(
        own_kernel,
        grid=(QUADS,),
        in_specs=[packed_spec(own), weight_spec(0), weight_spec(1), weight_spec(2)],
        out_specs=[QUERY_SPEC, *STATE_SPECS],
        out_shape=[jax.ShapeDtypeStruct((CHUNKS, 2 * ROWS, LANES), BF16), *STATE_SHAPES],
        compiler_params=LIMIT,
        cost_estimate=cost(3, 8),
        name="own_block",
    )(own, w_qkv, w_qkv, w_qkv)


def absorb_side(blocks, own_row, queries_ref, wk_ref, wv_ref, state):
    frames = jnp.concatenate([unpacked(block) for block in blocks], axis=0)
    keys = projected(frames, wk_ref)
    values = projected(frames, wv_ref)
    columns = jnp.concatenate([id_column(id_row(block)) for block in blocks], axis=0)
    absorb(queries_ref, keys, values, columns == own_row, *state, False)


def absorb_both(own_ref, left, right, queries_ref, wk_ref, wv_ref, state):
    own_row = id_row((own_ref, 0))
    left_needed = jnp.max(id_row(left[0])) == jnp.min(own_row)
    right_needed = jnp.min(id_row(right[0])) == jnp.max(own_row)

    @pl.when(left_needed)
    def _():
        absorb_side(left, own_row, queries_ref, wk_ref, wv_ref, state)

    @pl.when(right_needed)
    def _():
        absorb_side(right, own_row, queries_ref, wk_ref, wv_ref, state)


def located(refs, places):
    return [(refs[i], slot) for i, slot in places]


def absorb_stage(own, blocks, left, right, queries, w_qkv, state):
    count = len(blocks)

    def kernel(own_ref, *refs):
        block_refs, refs = refs[:count], refs[count:]
        queries_ref, wk_ref, wv_ref, old_tops, old_sums, old_acc, tops_ref, sums_ref, acc_ref = refs
        tops_ref[...] = old_tops[...]
        sums_ref[...] = old_sums[...]
        acc_ref[...] = old_acc[...]
        state_refs = (tops_ref, sums_ref, acc_ref)
        absorb_both(
            own_ref, located(block_refs, left), located(block_refs, right),
            queries_ref, wk_ref, wv_ref, state_refs,
        )

    return pl.pallas_call(
        kernel,
        grid=(QUADS,),
        in_specs=[packed_spec(own)]
        + [packed_spec(block) for block in blocks]
        + [QUERY_SPEC, weight_spec(1), weight_spec(2), *STATE_SPECS],
        out_specs=list(STATE_SPECS),
        out_shape=list(STATE_SHAPES),
        compiler_params=LIMIT,
        cost_estimate=cost(len(left) + len(right), 8),
        name="absorb_stage",
    )(own, *blocks, queries, w_qkv, w_qkv, *state)


def last_stage(own, blocks, left, right, queries, w_qkv, state, frames, w_out):
    count = len(blocks)

    def kernel(own_ref, *refs):
        block_refs, refs = refs[:count], refs[count:]
        queries_ref, wk_ref, wv_ref, old_tops, old_sums, old_acc = refs[:6]
        frames_ref, wout_ref, attended_ref, out_ref, tops_ref, sums_ref, acc_ref, total_ref = refs[6:]
        quad = pl.program_id(0)
        tops_ref[...] = old_tops[...]
        sums_ref[...] = old_sums[...]
        acc_ref[...] = old_acc[...]
        state_refs = (tops_ref, sums_ref, acc_ref)
        absorb_both(
            own_ref, located(block_refs, left), located(block_refs, right),
            queries_ref, wk_ref, wv_ref, state_refs,
        )
        for h in range(4):
            rows = slice(h * HALF, (h + 1) * HALF)
            attended_ref[rows, :] = (acc_ref[rows, :] / sums_ref[h : h + 1, :]).astype(BF16)
        term = jnp.dot(jnp.transpose(attended_ref[...]), wout_ref[...], preferred_element_type=F32)

        @pl.when(quad == 0)
        def _():
            total_ref[...] = frames_ref[...].astype(F32) + term

        @pl.when(quad > 0)
        def _():
            total_ref[...] += term

        @pl.when(quad == QUADS - 1)
        def _():
            out_ref[...] = total_ref[...].astype(BF16)

    return pl.pallas_call(
        kernel,
        grid=(QUADS,),
        in_specs=[packed_spec(own)]
        + [packed_spec(block) for block in blocks]
        + [QUERY_SPEC, weight_spec(1), weight_spec(2), *STATE_SPECS]
        + [
            pl.BlockSpec((ROWS, WIDTH), lambda j: (0, 0)),
            pl.BlockSpec((QUAD, WIDTH), lambda j: (j, 0)),
        ],
        out_specs=[
            pl.BlockSpec((QUAD, LANES), lambda j: (j, 0)),
            pl.BlockSpec((ROWS, WIDTH), lambda j: (0, 0)),
        ],
        out_shape=[
            jax.ShapeDtypeStruct((WIDTH, LANES), BF16),
            jax.ShapeDtypeStruct((ROWS, WIDTH), BF16),
        ],
        scratch_shapes=[
            pltpu.VMEM((8, LANES), F32),
            pltpu.VMEM((8, LANES), F32),
            pltpu.VMEM((QUAD, LANES), F32),
            pltpu.VMEM((ROWS, WIDTH), F32),
        ],
        compiler_params=LIMIT,
        cost_estimate=cost(len(left) + len(right) + 1, 10),
        name="last_stage",
    )(own, *blocks, queries, w_qkv, w_qkv, *state, frames, w_out)


def grad_kernel(attended_ref, cotangent_ref, out_ref):
    attended = jnp.concatenate([attended_ref[p] for p in range(CHUNKS)], axis=1)
    product = jnp.dot(attended, cotangent_ref[...], preferred_element_type=F32).astype(BF16)
    for half in range(2):
        out_ref[half] = product[:, half * LANES : (half + 1) * LANES]


def grad_product(attended, cotangent):
    return pl.pallas_call(
        grad_kernel,
        grid=(QUADS,),
        in_specs=[
            pl.BlockSpec((CHUNKS, LANES, ROWS), lambda j: (0, 0, 0)),
            pl.BlockSpec((CHUNKS * ROWS, QUAD), lambda j: (0, j)),
        ],
        out_specs=pl.BlockSpec((2, LANES, LANES), lambda j: (j, 0, 0)),
        out_shape=jax.ShapeDtypeStruct((CHUNKS, LANES, LANES), BF16),
        compiler_params=LIMIT,
        name="grad_product",
    )(attended, cotangent)


def gathered_over_dp(block):
    n_dp = lax.axis_size("dp")
    chips = n_dp // 2

    def turned(distance):
        route = [((2 * x + c), 2 * ((x + distance) % chips) + c) for x in range(chips) for c in range(2)]
        return lax.ppermute(block, "dp", route)

    ring = [block, turned(1), turned(2), turned(3)]
    mine = jnp.concatenate(ring, axis=0)
    theirs = lax.ppermute(mine, "dp", [(i, i ^ 1) for i in range(n_dp)])
    return mine, theirs


def local(frames, segment_ids, norm_gain, w_qkv, w_out, cotangent):
    n_dp = lax.axis_size("dp")
    n_seq = lax.axis_size("seq")
    frames = frames[0]
    own = normalize(frames, segment_ids, norm_gain[None, :])

    left1, right1 = shifted(own, 1), shifted(own, -1)
    queries, *state = own_block(own, w_qkv)
    trio = jnp.concatenate([left1, own, right1], axis=0)
    left_trio, right_trio = shifted(trio, 4), shifted(trio, -4)
    left2, right2 = shifted(left1, 1), shifted(right1, -1)
    state = absorb_stage(
        own, (left1, left2, right1, right2), ((0, 0), (1, 0)), ((2, 0), (3, 0)), queries, w_qkv, state
    )
    mine, theirs = gathered_over_dp(cotangent[0])

    left2, right2, left_trio, right_trio = lax.optimization_barrier(
        (left2, right2, left_trio, right_trio)
    )
    left6, right6 = shifted(left2, 4), shifted(right2, -4)
    state = absorb_stage(
        own, (left_trio, right_trio), ((0, 2), (0, 1), (0, 0)), ((1, 0), (1, 1), (1, 2)),
        queries, w_qkv, state,
    )
    attended, block_out = last_stage(
        own, (left6, right6), ((0, 0),), ((1, 0),), queries, w_qkv, state, frames, w_out
    )

    pieces = lax.all_to_all(attended, "dp", 0, 0, tiled=True).reshape(n_dp, LANES, ROWS)
    chip = lax.axis_index("dp") // 2
    core = lax.axis_index("dp") % 2
    chips = n_dp // 2
    order = [2 * ((chip - d) % chips) + core for d in range(chips)]
    order += [2 * ((chip - d) % chips) + 1 - core for d in range(chips)]
    pieces = jnp.take(pieces, jnp.stack(order), axis=0)
    share = grad_product(pieces, jnp.concatenate([mine, theirs], axis=0))
    rows = LANES * CHUNKS // n_seq
    parts = lax.all_to_all(share.reshape(n_seq, rows, LANES), "seq", 0, 0, tiled=True)
    grad_scale = (n_dp * n_seq * ROWS) ** (-0.5)
    block = jnp.sum(parts.astype(F32), axis=0) * grad_scale
    inner = n_seq // n_dp
    route = [
        (p * n_seq + q * inner + r, q * n_seq + p * inner + r)
        for p in range(n_dp)
        for q in range(n_dp)
        for r in range(inner)
    ]
    return (block_out[None], lax.ppermute(block, ("dp", "seq"), route))


def solution(mesh):
    placed = (P("dp", "seq", None), P("dp", "seq"), P(), P(), P(), P("dp", "seq", None))
    return jax.shard_map(
        local,
        mesh=mesh,
        in_specs=placed,
        out_specs=(P("dp", "seq", None), P("seq", "dp")),
        check_vma=False,
    )
```

```python
import jax
import jax.numpy as jnp
from jax import lax
from jax.experimental import pallas as pl
from jax.experimental.pallas import tpu as pltpu
from jax.sharding import PartitionSpec as P

ROWS = 128
LANES = 128
HALF = 64
WIDTH = 1024
CHUNKS = WIDTH // LANES
PACKED = WIDTH + 16
QUAD = 256
QUADS = WIDTH // QUAD
NEG_BIG = -1e30
EPSILON = 1e-05
LOG2E = 1.4426950408889634
AHEAD = 2
F32 = jnp.float32
BF16 = jnp.bfloat16
LIMIT = pltpu.CompilerParams(vmem_limit_bytes=40 * 1024 * 1024)


def shifted(block, distance):
    n_seq = lax.axis_size("seq")
    route = [(i, (i + distance) % n_seq) for i in range(n_seq)]
    return lax.ppermute(block, "seq", route)


def norm_kernel(frames_ref, ids_ref, gain_ref, packed_ref):
    float_frames = frames_ref[...].astype(F32)
    average = jnp.mean(float_frames, axis=-1, keepdims=True)
    centered = float_frames - average
    variance = jnp.mean(centered * centered, axis=-1, keepdims=True)
    normed = (centered * lax.rsqrt(variance + EPSILON) * gain_ref[...]).astype(BF16)
    for c in range(CHUNKS):
        packed_ref[c * ROWS : (c + 1) * ROWS, :] = normed[:, c * LANES : (c + 1) * LANES]
    ids = (ids_ref[...] + 1).astype(F32)
    packed_ref[WIDTH:PACKED, :] = jnp.broadcast_to(ids, (16, LANES)).astype(BF16)


def normalize(frames, ids, gain):
    return pl.pallas_call(
        norm_kernel,
        out_shape=jax.ShapeDtypeStruct((PACKED, LANES), BF16),
        compiler_params=pltpu.CompilerParams(vmem_limit_bytes=60 * 1024 * 1024),
        name="layer_norm",
    )(frames, ids, gain)


def unpacked(block):
    ref, slot = block
    base = slot * PACKED
    chunks = [ref[base + c * ROWS : base + (c + 1) * ROWS, :] for c in range(CHUNKS)]
    return jnp.concatenate(chunks, axis=1)


def id_row(block):
    ref, slot = block
    base = slot * PACKED + WIDTH
    return ref[base : base + 16, :].astype(F32)[0:1, :]


def id_column(row):
    across = lax.broadcasted_iota(jnp.int32, (ROWS, LANES), 1)
    down = lax.broadcasted_iota(jnp.int32, (ROWS, LANES), 0)
    return jnp.sum(jnp.where(across == down, row, 0.0), axis=1, keepdims=True)


def projected(frames, weight_ref, section, quad):
    at = section * WIDTH + quad * QUAD
    block = weight_ref[:, at : at + QUAD]
    return jnp.dot(frames, block, preferred_element_type=F32).astype(BF16)


def absorb(frames, bias, queries_ref, weight_ref, state, first):
    tops_ref, sums_ref, acc_ref = state
    both = jnp.concatenate([bias, bias], axis=1)
    pairs = 2 * QUADS
    keys, flipped, waiting = {}, {}, []

    def score(index):
        quad, at = index // 2, (index % 2) * LANES
        if quad not in keys:
            keys[quad] = projected(frames, weight_ref, 1, quad)
            flipped[quad] = jnp.transpose(projected(frames, weight_ref, 2, quad))
        part = keys[quad][:, at : at + LANES]
        return jnp.dot(part, queries_ref[index], preferred_element_type=F32) + both

    for index in range(pairs + AHEAD):
        if index < pairs:
            waiting.append(score(index))
        if index < AHEAD:
            continue
        pair = index - AHEAD
        heads = (2 * pair, 2 * pair + 1)
        scores = waiting[pair]
        waiting[pair] = None
        top = jnp.max(scores, axis=0, keepdims=True)
        if not first:
            old_top = jnp.concatenate([tops_ref[h : h + 1, :] for h in heads], axis=1)
            old_sum = jnp.concatenate([sums_ref[h : h + 1, :] for h in heads], axis=1)
            top = jnp.maximum(old_top, top)
            rescale = jnp.exp2((old_top - top) * LOG2E)
        weights = jnp.exp2((scores - top) * LOG2E)
        total = jnp.sum(weights, axis=0, keepdims=True)
        at = (pair % 2) * LANES
        values = flipped[pair // 2][at : at + LANES, :]
        mixed = jnp.dot(values, weights.astype(BF16), preferred_element_type=F32)
        if not first:
            total = old_sum * rescale + total
        for k, h in enumerate(heads):
            lanes = slice(k * LANES, (k + 1) * LANES)
            rows = slice(h * HALF, (h + 1) * HALF)
            term = mixed[k * HALF : (k + 1) * HALF, lanes]
            if not first:
                term = acc_ref[rows, :] * rescale[:, lanes] + term
            acc_ref[rows, :] = term
            tops_ref[h : h + 1, :] = top[:, lanes]
            sums_ref[h : h + 1, :] = total[:, lanes]


def bias_of(blocks, own_row):
    columns = jnp.concatenate([id_column(id_row(block)) for block in blocks], axis=0)
    return jnp.where(columns == own_row, 0.0, NEG_BIG)


def own_kernel(own_ref, weight_ref, queries_ref, *state):
    frames = unpacked((own_ref, 0))
    row = id_row((own_ref, 0))
    for quad in range(QUADS):
        queries = projected(frames, weight_ref, 0, quad) * jnp.asarray(0.125, BF16)
        flipped = jnp.transpose(queries)
        zeros = jnp.zeros((HALF, ROWS), BF16)
        for pair in range(2):
            index = 2 * quad + pair
            at = pair * LANES
            queries_ref[index, 0:HALF, 0:ROWS] = flipped[at : at + HALF, :]
            queries_ref[index, 0:HALF, ROWS:] = zeros
            queries_ref[index, HALF:, 0:ROWS] = zeros
            queries_ref[index, HALF:, ROWS:] = flipped[at + HALF : at + LANES, :]
    absorb(frames, bias_of(((own_ref, 0),), row), queries_ref, weight_ref, state, True)


STATE_SHAPES = (
    jax.ShapeDtypeStruct((2 * CHUNKS, LANES), F32),
    jax.ShapeDtypeStruct((2 * CHUNKS, LANES), F32),
    jax.ShapeDtypeStruct((WIDTH, LANES), F32),
)


def cost(blocks, mib):
    return pl.CostEstimate(
        flops=2 * blocks * ROWS * WIDTH * 2 * WIDTH, bytes_accessed=mib << 20, transcendentals=0
    )


def own_block(own, w_qkv):
    return pl.pallas_call(
        own_kernel,
        out_shape=[jax.ShapeDtypeStruct((CHUNKS, LANES, 2 * ROWS), BF16), *STATE_SHAPES],
        compiler_params=LIMIT,
        cost_estimate=cost(3, 8),
        name="own_block",
    )(own, w_qkv)


def absorb_both(own_ref, left, right, queries_ref, weight_ref, state):
    own_row = id_row((own_ref, 0))
    left_needed = jnp.max(id_row(left[0])) == jnp.min(own_row)
    right_needed = jnp.min(id_row(right[0])) == jnp.max(own_row)

    @pl.when(left_needed | right_needed)
    def _():
        blocks = (*left, *right)
        frames = jnp.concatenate([unpacked(block) for block in blocks], axis=0)
        absorb(frames, bias_of(blocks, own_row), queries_ref, weight_ref, state, False)


def located(refs, places):
    return [(refs[i], slot) for i, slot in places]


def copied(old_state, state):
    for old, new in zip(old_state, state):
        new[...] = old[...]


def absorb_stage(own, blocks, left, right, queries, w_qkv, state):
    count = len(blocks)

    def kernel(own_ref, *refs):
        block_refs, refs = refs[:count], refs[count:]
        queries_ref, weight_ref = refs[:2]
        copied(refs[2:5], refs[5:8])
        absorb_both(
            own_ref, located(block_refs, left), located(block_refs, right), queries_ref, weight_ref, refs[5:8]
        )

    return pl.pallas_call(
        kernel,
        out_shape=list(STATE_SHAPES),
        compiler_params=LIMIT,
        cost_estimate=cost(len(left) + len(right), 8),
        name="absorb_stage",
    )(own, *blocks, queries, w_qkv, *state)


def last_stage(own, blocks, left, right, queries, w_qkv, state, frames, w_out):
    count = len(blocks)

    def kernel(own_ref, *refs):
        block_refs, refs = refs[:count], refs[count:]
        queries_ref, weight_ref = refs[:2]
        frames_ref, wout_ref, attended_ref, out_ref = refs[5:9]
        state_refs = refs[9:12]
        copied(refs[2:5], state_refs)
        absorb_both(
            own_ref, located(block_refs, left), located(block_refs, right), queries_ref, weight_ref, state_refs
        )
        _, sums_ref, acc_ref = state_refs
        for h in range(2 * CHUNKS):
            rows = slice(h * HALF, (h + 1) * HALF)
            attended_ref[rows, :] = (acc_ref[rows, :] / sums_ref[h : h + 1, :]).astype(BF16)
        attended = jnp.concatenate(
            [jnp.transpose(attended_ref[c * LANES : (c + 1) * LANES, :]) for c in range(CHUNKS)], axis=1
        )
        product = jnp.dot(attended, wout_ref[...], preferred_element_type=F32)
        out_ref[...] = (frames_ref[...].astype(F32) + product).astype(BF16)

    return pl.pallas_call(
        kernel,
        out_shape=[
            jax.ShapeDtypeStruct((WIDTH, LANES), BF16),
            jax.ShapeDtypeStruct((ROWS, WIDTH), BF16),
        ],
        scratch_shapes=[pltpu.VMEM(shape.shape, F32) for shape in STATE_SHAPES],
        compiler_params=LIMIT,
        cost_estimate=cost(len(left) + len(right) + 1, 10),
        name="last_stage",
    )(own, *blocks, queries, w_qkv, *state, frames, w_out)


def grad_kernel(attended_ref, cotangent_ref, out_ref):
    attended = jnp.concatenate([attended_ref[p] for p in range(CHUNKS)], axis=1)
    product = jnp.dot(attended, cotangent_ref[...], preferred_element_type=F32).astype(BF16)
    for half in range(2):
        out_ref[half] = product[:, half * LANES : (half + 1) * LANES]


def grad_product(attended, cotangent):
    return pl.pallas_call(
        grad_kernel,
        grid=(QUADS,),
        in_specs=[
            pl.BlockSpec((CHUNKS, LANES, ROWS), lambda j: (0, 0, 0)),
            pl.BlockSpec((CHUNKS * ROWS, QUAD), lambda j: (0, j)),
        ],
        out_specs=pl.BlockSpec((2, LANES, LANES), lambda j: (j, 0, 0)),
        out_shape=jax.ShapeDtypeStruct((CHUNKS, LANES, LANES), BF16),
        compiler_params=LIMIT,
        name="grad_product",
    )(attended, cotangent)


def local(frames, segment_ids, norm_gain, w_qkv, w_out, cotangent):
    n_dp = lax.axis_size("dp")
    n_seq = lax.axis_size("seq")
    frames = frames[0]
    own = normalize(frames, segment_ids, norm_gain[None, :])

    left1, right1 = shifted(own, 1), shifted(own, -1)
    left4, right4 = shifted(own, 4), shifted(own, -4)
    queries, *state = own_block(own, w_qkv)
    left1, right1, left4, right4, queries = lax.optimization_barrier(
        (left1, right1, left4, right4, queries)
    )
    near = jnp.concatenate([left1, right1], axis=0)
    left_two, right_two = shifted(near, 4), shifted(near, -4)
    left2, right2 = shifted(left1, 1), shifted(right1, -1)
    cotangent, near = lax.optimization_barrier((cotangent, near))
    copies = jnp.broadcast_to(cotangent, (n_dp, *cotangent.shape[1:]))
    all_grads = lax.all_to_all(copies, "dp", 0, 0, tiled=True).reshape(n_dp * ROWS, WIDTH)

    state = absorb_stage(
        own, (left1, left4, right1, right4), ((0, 0), (1, 0)), ((2, 0), (3, 0)), queries, w_qkv, state
    )
    state = absorb_stage(own, (left2, right2), ((0, 0),), ((1, 0),), queries, w_qkv, state)
    left2, right2, left_two, right_two = lax.optimization_barrier((left2, right2, left_two, right_two))
    left6, right6 = shifted(left2, 4), shifted(right2, -4)
    state = absorb_stage(
        own, (left_two, right_two), ((0, 1), (0, 0)), ((1, 0), (1, 1)), queries, w_qkv, state
    )
    attended, block_out = last_stage(
        own, (left6, right6), ((0, 0),), ((1, 0),), queries, w_qkv, state, frames, w_out
    )

    pieces = lax.all_to_all(attended, "dp", 0, 0, tiled=True).reshape(n_dp, LANES, ROWS)
    share = grad_product(pieces, all_grads)
    rows = LANES * CHUNKS // n_seq
    parts = lax.all_to_all(share.reshape(n_seq, rows, LANES), "seq", 0, 0, tiled=True)
    grad_scale = (n_dp * n_seq * ROWS) ** (-0.5)
    block = jnp.sum(parts.astype(F32), axis=0) * grad_scale
    inner = n_seq // n_dp
    route = [
        (p * n_seq + q * inner + r, q * n_seq + p * inner + r)
        for p in range(n_dp)
        for q in range(n_dp)
        for r in range(inner)
    ]
    return (block_out[None], lax.ppermute(block, ("dp", "seq"), route))


def solution(mesh):
    placed = (P("dp", "seq", None), P("dp", "seq"), P(), P(), P(), P("dp", "seq", None))
    return jax.shard_map(
        local,
        mesh=mesh,
        in_specs=placed,
        out_specs=(P("dp", "seq", None), P("seq", "dp")),
        check_vma=False,
    )
```

```python
import jax
import jax.numpy as jnp
from jax import lax
from jax.experimental import pallas as pl
from jax.experimental.pallas import tpu as pltpu
from jax.sharding import PartitionSpec as P

ROWS = 128
LANES = 128
HALF = 64
WIDTH = 1024
CHUNKS = WIDTH // LANES
PACKED = WIDTH + 16
QUAD = 256
QUADS = WIDTH // QUAD
NEG_BIG = -1e30
EPSILON = 1e-05
LOG2E = 1.4426950408889634
AHEAD = 2
F32 = jnp.float32
BF16 = jnp.bfloat16
LIMIT = pltpu.CompilerParams(vmem_limit_bytes=40 * 1024 * 1024)


def shifted(block, distance):
    n_seq = lax.axis_size("seq")
    route = [(i, (i + distance) % n_seq) for i in range(n_seq)]
    return lax.ppermute(block, "seq", route)


def norm_kernel(frames_ref, ids_ref, gain_ref, packed_ref):
    float_frames = frames_ref[...].astype(F32)
    average = jnp.mean(float_frames, axis=-1, keepdims=True)
    centered = float_frames - average
    variance = jnp.mean(centered * centered, axis=-1, keepdims=True)
    normed = (centered * lax.rsqrt(variance + EPSILON) * gain_ref[...]).astype(BF16)
    for c in range(CHUNKS):
        packed_ref[c * ROWS : (c + 1) * ROWS, :] = normed[:, c * LANES : (c + 1) * LANES]
    ids = (ids_ref[...] + 1).astype(F32)
    packed_ref[WIDTH:PACKED, :] = jnp.broadcast_to(ids, (16, LANES)).astype(BF16)


def normalize(frames, ids, gain):
    return pl.pallas_call(
        norm_kernel,
        out_shape=jax.ShapeDtypeStruct((PACKED, LANES), BF16),
        compiler_params=pltpu.CompilerParams(vmem_limit_bytes=60 * 1024 * 1024),
        name="layer_norm",
    )(frames, ids, gain)


def unpacked(block):
    ref, slot = block
    base = slot * PACKED
    chunks = [ref[base + c * ROWS : base + (c + 1) * ROWS, :] for c in range(CHUNKS)]
    return jnp.concatenate(chunks, axis=1)


def id_row(block):
    ref, slot = block
    base = slot * PACKED + WIDTH
    return ref[base : base + 16, :].astype(F32)[0:1, :]


def id_column(row):
    across = lax.broadcasted_iota(jnp.int32, (ROWS, LANES), 1)
    down = lax.broadcasted_iota(jnp.int32, (ROWS, LANES), 0)
    return jnp.sum(jnp.where(across == down, row, 0.0), axis=1, keepdims=True)


def projected(frames, weight_ref, section, quad):
    at = section * WIDTH + quad * QUAD
    block = weight_ref[:, at : at + QUAD]
    return jnp.dot(frames, block, preferred_element_type=F32).astype(BF16)


def absorb(frames, bias, queries_ref, weight_ref, state, first):
    tops_ref, sums_ref, acc_ref = state
    both = jnp.concatenate([bias, bias], axis=1)
    pairs = 2 * QUADS
    keys, flipped, waiting = {}, {}, []

    def score(index):
        quad, at = index // 2, (index % 2) * LANES
        if quad not in keys:
            keys[quad] = projected(frames, weight_ref, 1, quad)
            flipped[quad] = jnp.transpose(projected(frames, weight_ref, 2, quad))
        part = keys[quad][:, at : at + LANES]
        return jnp.dot(part, queries_ref[index], preferred_element_type=F32) + both

    for index in range(pairs + AHEAD):
        if index < pairs:
            waiting.append(score(index))
        if index < AHEAD:
            continue
        pair = index - AHEAD
        heads = (2 * pair, 2 * pair + 1)
        scores = waiting[pair]
        waiting[pair] = None
        top = jnp.max(scores, axis=0, keepdims=True)
        if not first:
            old_top = jnp.concatenate([tops_ref[h : h + 1, :] for h in heads], axis=1)
            old_sum = jnp.concatenate([sums_ref[h : h + 1, :] for h in heads], axis=1)
            top = jnp.maximum(old_top, top)
            rescale = jnp.exp2((old_top - top) * LOG2E)
        weights = jnp.exp2((scores - top) * LOG2E)
        total = jnp.sum(weights, axis=0, keepdims=True)
        at = (pair % 2) * LANES
        values = flipped[pair // 2][at : at + LANES, :]
        mixed = jnp.dot(values, weights.astype(BF16), preferred_element_type=F32)
        if not first:
            total = old_sum * rescale + total
        for k, h in enumerate(heads):
            lanes = slice(k * LANES, (k + 1) * LANES)
            rows = slice(h * HALF, (h + 1) * HALF)
            term = mixed[k * HALF : (k + 1) * HALF, lanes]
            if not first:
                term = acc_ref[rows, :] * rescale[:, lanes] + term
            acc_ref[rows, :] = term
            tops_ref[h : h + 1, :] = top[:, lanes]
            sums_ref[h : h + 1, :] = total[:, lanes]


def bias_of(blocks, own_row):
    columns = jnp.concatenate([id_column(id_row(block)) for block in blocks], axis=0)
    return jnp.where(columns == own_row, 0.0, NEG_BIG)


def own_kernel(own_ref, weight_ref, queries_ref, *state):
    frames = unpacked((own_ref, 0))
    row = id_row((own_ref, 0))
    for quad in range(QUADS):
        queries = projected(frames, weight_ref, 0, quad) * jnp.asarray(0.125, BF16)
        flipped = jnp.transpose(queries)
        zeros = jnp.zeros((HALF, ROWS), BF16)
        for pair in range(2):
            index = 2 * quad + pair
            at = pair * LANES
            queries_ref[index, 0:HALF, 0:ROWS] = flipped[at : at + HALF, :]
            queries_ref[index, 0:HALF, ROWS:] = zeros
            queries_ref[index, HALF:, 0:ROWS] = zeros
            queries_ref[index, HALF:, ROWS:] = flipped[at + HALF : at + LANES, :]
    absorb(frames, bias_of(((own_ref, 0),), row), queries_ref, weight_ref, state, True)


STATE_SHAPES = (
    jax.ShapeDtypeStruct((2 * CHUNKS, LANES), F32),
    jax.ShapeDtypeStruct((2 * CHUNKS, LANES), F32),
    jax.ShapeDtypeStruct((WIDTH, LANES), F32),
)


def cost(blocks, mib):
    return pl.CostEstimate(
        flops=2 * blocks * ROWS * WIDTH * 2 * WIDTH, bytes_accessed=mib << 20, transcendentals=0
    )


def own_block(own, w_qkv):
    return pl.pallas_call(
        own_kernel,
        out_shape=[jax.ShapeDtypeStruct((CHUNKS, LANES, 2 * ROWS), BF16), *STATE_SHAPES],
        compiler_params=LIMIT,
        cost_estimate=cost(3, 8),
        name="own_block",
    )(own, w_qkv)


def absorb_both(own_ref, left, right, queries_ref, weight_ref, state):
    own_row = id_row((own_ref, 0))
    left_needed = jnp.max(id_row(left[0])) == jnp.min(own_row)
    right_needed = jnp.min(id_row(right[0])) == jnp.max(own_row)

    @pl.when(left_needed | right_needed)
    def _():
        blocks = (*left, *right)
        frames = jnp.concatenate([unpacked(block) for block in blocks], axis=0)
        absorb(frames, bias_of(blocks, own_row), queries_ref, weight_ref, state, False)


def located(refs, places):
    return [(refs[i], slot) for i, slot in places]


def copied(old_state, state):
    for old, new in zip(old_state, state):
        new[...] = old[...]


def absorb_stage(own, blocks, left, right, queries, w_qkv, state):
    count = len(blocks)

    def kernel(own_ref, *refs):
        block_refs, refs = refs[:count], refs[count:]
        queries_ref, weight_ref = refs[:2]
        copied(refs[2:5], refs[5:8])
        absorb_both(
            own_ref, located(block_refs, left), located(block_refs, right), queries_ref, weight_ref, refs[5:8]
        )

    return pl.pallas_call(
        kernel,
        out_shape=list(STATE_SHAPES),
        compiler_params=LIMIT,
        cost_estimate=cost(len(left) + len(right), 8),
        name="absorb_stage",
    )(own, *blocks, queries, w_qkv, *state)


def last_stage(own, blocks, left, right, queries, w_qkv, state, frames, w_out):
    count = len(blocks)

    def kernel(own_ref, *refs):
        block_refs, refs = refs[:count], refs[count:]
        queries_ref, weight_ref = refs[:2]
        frames_ref, wout_ref, attended_ref, out_ref = refs[5:9]
        state_refs = refs[9:12]
        copied(refs[2:5], state_refs)
        absorb_both(
            own_ref, located(block_refs, left), located(block_refs, right), queries_ref, weight_ref, state_refs
        )
        _, sums_ref, acc_ref = state_refs
        for h in range(2 * CHUNKS):
            rows = slice(h * HALF, (h + 1) * HALF)
            attended_ref[rows, :] = (acc_ref[rows, :] / sums_ref[h : h + 1, :]).astype(BF16)
        attended = jnp.concatenate(
            [jnp.transpose(attended_ref[c * LANES : (c + 1) * LANES, :]) for c in range(CHUNKS)], axis=1
        )
        product = jnp.dot(attended, wout_ref[...], preferred_element_type=F32)
        out_ref[...] = (frames_ref[...].astype(F32) + product).astype(BF16)

    return pl.pallas_call(
        kernel,
        out_shape=[
            jax.ShapeDtypeStruct((WIDTH, LANES), BF16),
            jax.ShapeDtypeStruct((ROWS, WIDTH), BF16),
        ],
        scratch_shapes=[pltpu.VMEM(shape.shape, F32) for shape in STATE_SHAPES],
        compiler_params=LIMIT,
        cost_estimate=cost(len(left) + len(right) + 1, 10),
        name="last_stage",
    )(own, *blocks, queries, w_qkv, *state, frames, w_out)


def grad_kernel(order_ref, attended_ref, *refs):
    grads, out_ref = refs[:-1], refs[-1]
    attended = jnp.concatenate([attended_ref[order_ref[i]] for i in range(len(grads))], axis=1)
    for quad in range(QUADS):
        at = slice(quad * QUAD, (quad + 1) * QUAD)
        block = jnp.concatenate([ref[:, at] for ref in grads], axis=0)
        product = jnp.dot(attended, block, preferred_element_type=F32).astype(BF16)
        for half in range(2):
            out_ref[2 * quad + half] = product[:, half * LANES : (half + 1) * LANES]


def grad_product(order, attended, grads):
    vmem = pl.BlockSpec(memory_space=pltpu.VMEM)
    return pl.pallas_call(
        grad_kernel,
        in_specs=[pl.BlockSpec(memory_space=pltpu.SMEM)] + [vmem] * (1 + len(grads)),
        out_shape=jax.ShapeDtypeStruct((CHUNKS, LANES, LANES), BF16),
        compiler_params=LIMIT,
        name="grad_product",
    )(order, attended, *grads)


def chip_turned(block, distance):
    n_dp = lax.axis_size("dp")
    route = [(i, (i + 2 * distance) % n_dp) for i in range(n_dp)]
    return lax.ppermute(block, "dp", route)


def core_swapped(block):
    return lax.ppermute(block, "dp", [(i, i ^ 1) for i in range(lax.axis_size("dp"))])


def gathered_order():
    n_dp = lax.axis_size("dp")
    table = []
    for place in range(n_dp):
        ring = [(place + n_dp - 2 * d) % n_dp for d in range(n_dp // 2)]
        table.append(ring + [i ^ 1 for i in ring])
    return lax.dynamic_index_in_dim(jnp.asarray(table, jnp.int32), lax.axis_index("dp"), 0, False)


def local(frames, segment_ids, norm_gain, w_qkv, w_out, cotangent):
    n_dp = lax.axis_size("dp")
    n_seq = lax.axis_size("seq")
    frames = frames[0]
    own = normalize(frames, segment_ids, norm_gain[None, :])

    left1, right1 = shifted(own, 1), shifted(own, -1)
    left4, right4 = shifted(own, 4), shifted(own, -4)
    cotangent = cotangent[0]
    ring = [chip_turned(cotangent, d) for d in range(1, n_dp // 2)]
    queries, *state = own_block(own, w_qkv)
    left1, right1, left4, right4, queries = lax.optimization_barrier(
        (left1, right1, left4, right4, queries)
    )
    near = jnp.concatenate([left1, right1], axis=0)
    left_two, right_two = shifted(near, 4), shifted(near, -4)
    left2, right2 = shifted(left1, 1), shifted(right1, -1)
    near, *ring = lax.optimization_barrier((near, *ring))
    grads = [cotangent, *ring, core_swapped(cotangent), *[core_swapped(block) for block in ring]]

    state = absorb_stage(
        own, (left1, left4, right1, right4), ((0, 0), (1, 0)), ((2, 0), (3, 0)), queries, w_qkv, state
    )
    state = absorb_stage(own, (left2, right2), ((0, 0),), ((1, 0),), queries, w_qkv, state)
    left2, right2, left_two, right_two = lax.optimization_barrier((left2, right2, left_two, right_two))
    left6, right6 = shifted(left2, 4), shifted(right2, -4)
    state = absorb_stage(
        own, (left_two, right_two), ((0, 1), (0, 0)), ((1, 0), (1, 1)), queries, w_qkv, state
    )
    attended, block_out = last_stage(
        own, (left6, right6), ((0, 0),), ((1, 0),), queries, w_qkv, state, frames, w_out
    )

    pieces = lax.all_to_all(attended, "dp", 0, 0, tiled=True).reshape(n_dp, LANES, ROWS)
    share = grad_product(gathered_order(), pieces, grads)
    rows = LANES * CHUNKS // n_seq
    parts = lax.all_to_all(share.reshape(n_seq, rows, LANES), "seq", 0, 0, tiled=True)
    grad_scale = (n_dp * n_seq * ROWS) ** (-0.5)
    block = jnp.sum(parts.astype(F32), axis=0) * grad_scale
    inner = n_seq // n_dp
    route = [
        (p * n_seq + q * inner + r, q * n_seq + p * inner + r)
        for p in range(n_dp)
        for q in range(n_dp)
        for r in range(inner)
    ]
    return (block_out[None], lax.ppermute(block, ("dp", "seq"), route))


def solution(mesh):
    placed = (P("dp", "seq", None), P("dp", "seq"), P(), P(), P(), P("dp", "seq", None))
    return jax.shard_map(
        local,
        mesh=mesh,
        in_specs=placed,
        out_specs=(P("dp", "seq", None), P("seq", "dp")),
        check_vma=False,
    )
```

```python
import jax
import jax.numpy as jnp
from jax import lax
from jax.experimental import pallas as pl
from jax.experimental.pallas import tpu as pltpu
from jax.sharding import Mesh, PartitionSpec as P

ROWS = 128
LANES = 128
HALF = 64
WIDTH = 1024
CHUNKS = WIDTH // LANES
PACKED = WIDTH + 16
QUAD = 256
QUADS = WIDTH // QUAD
SEQ = ("z", "y")
NEG_BIG = -1e30
EPSILON = 1e-05
N_SEQ = 32
N_Y = 4
N_CORE = 2
LOG2E = 1.4426950408889634
AHEAD = 2
F32 = jnp.float32
BF16 = jnp.bfloat16
LIMIT = pltpu.CompilerParams(vmem_limit_bytes=40 * 1024 * 1024)


def shifted(block, distance):
    n_seq = lax.axis_size(SEQ)
    route = [(i, (i + distance) % n_seq) for i in range(n_seq)]
    return lax.ppermute(block, SEQ, route)


def core_swapped(block):
    return lax.ppermute(block, "core", [(0, 1), (1, 0)])


def turned(block, distance):
    n = lax.axis_size("y")
    return lax.ppermute(block, "y", [(i, (i + distance) % n) for i in range(n)])


def gathered_order():
    n = lax.axis_size("y")
    table = [[(place + n - d) % n for d in range(n)] for place in range(n)]
    return lax.dynamic_index_in_dim(jnp.asarray(table, jnp.int32), lax.axis_index("y"), 0, False)


def norm_kernel(core_ref, frames_ref, ids_ref, gain_ref, cotangent_ref, packed_ref, mine_ref, theirs_ref):
    float_frames = frames_ref[...].astype(F32)
    average = jnp.mean(float_frames, axis=-1, keepdims=True)
    centered = float_frames - average
    variance = jnp.mean(centered * centered, axis=-1, keepdims=True)
    normed = (centered * lax.rsqrt(variance + EPSILON) * gain_ref[...]).astype(BF16)
    for c in range(CHUNKS):
        packed_ref[c * ROWS : (c + 1) * ROWS, :] = normed[:, c * LANES : (c + 1) * LANES]
    ids = (ids_ref[...] + 1).astype(F32)
    packed_ref[WIDTH:PACKED, :] = jnp.broadcast_to(ids, (16, LANES)).astype(BF16)
    first = core_ref[0] == 0
    for c in range(CHUNKS // 2):
        even = cotangent_ref[:, 2 * c * LANES : (2 * c + 1) * LANES]
        odd = cotangent_ref[:, (2 * c + 1) * LANES : (2 * c + 2) * LANES]
        at = slice(c * LANES, (c + 1) * LANES)
        mine_ref[:, at] = jnp.where(first, even, odd)
        theirs_ref[:, at] = jnp.where(first, odd, even)


def normalize(core, frames, ids, gain, cotangent):
    vmem = pl.BlockSpec(memory_space=pltpu.VMEM)
    half = jax.ShapeDtypeStruct((ROWS, WIDTH // 2), BF16)
    return pl.pallas_call(
        norm_kernel,
        in_specs=[pl.BlockSpec(memory_space=pltpu.SMEM), vmem, vmem, vmem, vmem],
        out_shape=[jax.ShapeDtypeStruct((PACKED, LANES), BF16), half, half],
        compiler_params=pltpu.CompilerParams(vmem_limit_bytes=60 * 1024 * 1024),
        name="layer_norm",
    )(core, frames, ids, gain, cotangent)


def unpacked(block):
    ref, slot = block
    base = slot * PACKED
    chunks = [ref[base + c * ROWS : base + (c + 1) * ROWS, :] for c in range(CHUNKS)]
    return jnp.concatenate(chunks, axis=1)


def id_row(block):
    ref, slot = block
    base = slot * PACKED + WIDTH
    return ref[base : base + 16, :].astype(F32)[0:1, :]


def id_column(row):
    across = lax.broadcasted_iota(jnp.int32, (ROWS, LANES), 1)
    down = lax.broadcasted_iota(jnp.int32, (ROWS, LANES), 0)
    return jnp.sum(jnp.where(across == down, row, 0.0), axis=1, keepdims=True)


def projected(frames, weight_ref, section, quad):
    at = section * WIDTH + quad * QUAD
    block = weight_ref[:, at : at + QUAD]
    return jnp.dot(frames, block, preferred_element_type=F32).astype(BF16)


def absorb(frames, bias, queries_ref, weight_ref, state, first):
    tops_ref, sums_ref, acc_ref = state
    both = jnp.concatenate([bias, bias], axis=1)
    pairs = 2 * QUADS
    keys, flipped, waiting = {}, {}, []

    def score(index):
        quad, at = index // 2, (index % 2) * LANES
        if quad not in keys:
            keys[quad] = projected(frames, weight_ref, 1, quad)
            flipped[quad] = jnp.transpose(projected(frames, weight_ref, 2, quad))
        part = keys[quad][:, at : at + LANES]
        return jnp.dot(part, queries_ref[index], preferred_element_type=F32) + both

    for index in range(pairs + AHEAD):
        if index < pairs:
            waiting.append(score(index))
        if index < AHEAD:
            continue
        pair = index - AHEAD
        heads = (2 * pair, 2 * pair + 1)
        scores = waiting[pair]
        waiting[pair] = None
        top = jnp.max(scores, axis=0, keepdims=True)
        if not first:
            old_top = jnp.concatenate([tops_ref[h : h + 1, :] for h in heads], axis=1)
            old_sum = jnp.concatenate([sums_ref[h : h + 1, :] for h in heads], axis=1)
            top = jnp.maximum(old_top, top)
            rescale = jnp.exp2((old_top - top) * LOG2E)
        weights = jnp.exp2((scores - top) * LOG2E)
        total = jnp.sum(weights, axis=0, keepdims=True)
        at = (pair % 2) * LANES
        values = flipped[pair // 2][at : at + LANES, :]
        mixed = jnp.dot(values, weights.astype(BF16), preferred_element_type=F32)
        if not first:
            total = old_sum * rescale + total
        for k, h in enumerate(heads):
            lanes = slice(k * LANES, (k + 1) * LANES)
            rows = slice(h * HALF, (h + 1) * HALF)
            term = mixed[k * HALF : (k + 1) * HALF, lanes]
            if not first:
                term = acc_ref[rows, :] * rescale[:, lanes] + term
            acc_ref[rows, :] = term
            tops_ref[h : h + 1, :] = top[:, lanes]
            sums_ref[h : h + 1, :] = total[:, lanes]


def bias_of(blocks, own_row):
    columns = jnp.concatenate([id_column(id_row(block)) for block in blocks], axis=0)
    return jnp.where(columns == own_row, 0.0, NEG_BIG)


def own_kernel(own_ref, weight_ref, queries_ref, *state):
    frames = unpacked((own_ref, 0))
    row = id_row((own_ref, 0))
    for quad in range(QUADS):
        queries = projected(frames, weight_ref, 0, quad) * jnp.asarray(0.125, BF16)
        flipped = jnp.transpose(queries)
        zeros = jnp.zeros((HALF, ROWS), BF16)
        for pair in range(2):
            index = 2 * quad + pair
            at = pair * LANES
            queries_ref[index, 0:HALF, 0:ROWS] = flipped[at : at + HALF, :]
            queries_ref[index, 0:HALF, ROWS:] = zeros
            queries_ref[index, HALF:, 0:ROWS] = zeros
            queries_ref[index, HALF:, ROWS:] = flipped[at + HALF : at + LANES, :]
    absorb(frames, bias_of(((own_ref, 0),), row), queries_ref, weight_ref, state, True)


STATE_SHAPES = (
    jax.ShapeDtypeStruct((2 * CHUNKS, LANES), F32),
    jax.ShapeDtypeStruct((2 * CHUNKS, LANES), F32),
    jax.ShapeDtypeStruct((WIDTH, LANES), F32),
)


def cost(blocks, mib):
    return pl.CostEstimate(
        flops=2 * blocks * ROWS * WIDTH * 2 * WIDTH, bytes_accessed=mib << 20, transcendentals=0
    )


def own_block(own, w_qkv):
    return pl.pallas_call(
        own_kernel,
        out_shape=[jax.ShapeDtypeStruct((CHUNKS, LANES, 2 * ROWS), BF16), *STATE_SHAPES],
        compiler_params=LIMIT,
        cost_estimate=cost(3, 8),
        name="own_block",
    )(own, w_qkv)


def absorb_both(own_ref, left, right, queries_ref, weight_ref, state):
    own_row = id_row((own_ref, 0))
    left_needed = jnp.max(id_row(left[0])) == jnp.min(own_row)
    right_needed = jnp.min(id_row(right[0])) == jnp.max(own_row)

    @pl.when(left_needed | right_needed)
    def _():
        blocks = (*left, *right)
        frames = jnp.concatenate([unpacked(block) for block in blocks], axis=0)
        absorb(frames, bias_of(blocks, own_row), queries_ref, weight_ref, state, False)


def located(refs, places):
    return [(refs[i], slot) for i, slot in places]


def copied(old_state, state):
    for old, new in zip(old_state, state):
        new[...] = old[...]


def absorb_stage(own, blocks, left, right, queries, w_qkv, state):
    count = len(blocks)

    def kernel(own_ref, *refs):
        block_refs, refs = refs[:count], refs[count:]
        queries_ref, weight_ref = refs[:2]
        copied(refs[2:5], refs[5:8])
        absorb_both(
            own_ref, located(block_refs, left), located(block_refs, right), queries_ref, weight_ref, refs[5:8]
        )

    return pl.pallas_call(
        kernel,
        out_shape=list(STATE_SHAPES),
        compiler_params=LIMIT,
        cost_estimate=cost(len(left) + len(right), 8),
        name="absorb_stage",
    )(own, *blocks, queries, w_qkv, *state)


def last_stage(own, blocks, left, right, queries, w_qkv, state, frames, w_out):
    count = len(blocks)

    def kernel(own_ref, *refs):
        block_refs, refs = refs[:count], refs[count:]
        queries_ref, weight_ref = refs[:2]
        frames_ref, wout_ref, attended_ref, out_ref = refs[5:9]
        state_refs = refs[9:12]
        copied(refs[2:5], state_refs)
        absorb_both(
            own_ref, located(block_refs, left), located(block_refs, right), queries_ref, weight_ref, state_refs
        )
        _, sums_ref, acc_ref = state_refs
        n_y, rows = attended_ref.shape[0], WIDTH // N_SEQ
        chunks = []
        for c in range(CHUNKS):
            parts = []
            for h in (2 * c, 2 * c + 1):
                parts.append((acc_ref[h * HALF : (h + 1) * HALF, :] / sums_ref[h : h + 1, :]).astype(BF16))
            chunk = jnp.concatenate(parts, axis=0)
            for k in range(LANES // rows):
                z, y = divmod(c * (LANES // rows) + k, n_y)
                attended_ref[y, z * rows : (z + 1) * rows, :] = chunk[k * rows : (k + 1) * rows, :]
            chunks.append(jnp.transpose(chunk))
        attended = jnp.concatenate(chunks, axis=1)
        product = jnp.dot(attended, wout_ref[...], preferred_element_type=F32)
        out_ref[...] = (frames_ref[...].astype(F32) + product).astype(BF16)

    return pl.pallas_call(
        kernel,
        out_shape=[
            jax.ShapeDtypeStruct((N_Y, WIDTH // N_Y, LANES), BF16),
            jax.ShapeDtypeStruct((ROWS, WIDTH), BF16),
        ],
        scratch_shapes=[pltpu.VMEM(shape.shape, F32) for shape in STATE_SHAPES],
        compiler_params=LIMIT,
        cost_estimate=cost(len(left) + len(right) + 1, 10),
        name="last_stage",
    )(own, *blocks, queries, w_qkv, *state, frames, w_out)


def grad_kernel(order_ref, own_ref, other_ref, *refs):
    grads, out_ref = refs[:-1], refs[-1]
    count = len(grads)
    attended = [ref[order_ref[i]] for i in range(count) for ref in (own_ref, other_ref)]
    attended = jnp.concatenate(attended, axis=1)
    for half in range(2):
        at = slice(half * QUAD, (half + 1) * QUAD)
        block = jnp.concatenate([ref[:, at] for ref in grads], axis=0)
        product = jnp.dot(attended, block, preferred_element_type=F32).astype(BF16)
        for k in range(2):
            out_ref[2 * half + k] = product[:, k * LANES : (k + 1) * LANES]


def grad_product(order, own, other, grads):
    vmem = pl.BlockSpec(memory_space=pltpu.VMEM)
    rows, columns = own.shape[1], grads[0].shape[1]
    return pl.pallas_call(
        grad_kernel,
        in_specs=[pl.BlockSpec(memory_space=pltpu.SMEM)] + [vmem] * (2 + len(grads)),
        out_shape=jax.ShapeDtypeStruct((columns // LANES, rows, LANES), BF16),
        compiler_params=LIMIT,
        name="grad_product",
    )(order, own, other, *grads)


def local(frames, segment_ids, norm_gain, w_qkv, w_out, cotangent):
    n_y = lax.axis_size("y")
    frames = frames[0]
    core = lax.axis_index("core").astype(jnp.int32).reshape(1)
    own, mine, theirs = normalize(core, frames, segment_ids, norm_gain[None, :], cotangent[0])

    left1, right1 = shifted(own, 1), shifted(own, -1)
    left4, right4 = shifted(own, 4), shifted(own, -4)
    received = core_swapped(theirs)
    queries, *state = own_block(own, w_qkv)
    left1, right1, queries = lax.optimization_barrier((left1, right1, queries))
    near = jnp.concatenate([left1, right1], axis=0)
    left2, right2 = shifted(left1, 1), shifted(right1, -1)
    left_two, right_two = shifted(near, 4), shifted(near, -4)
    state = absorb_stage(
        own, (left1, left4, right1, right4), ((0, 0), (1, 0)), ((2, 0), (3, 0)), queries, w_qkv, state
    )
    both = jnp.concatenate([mine, received], axis=0)
    both, left2, right2, *state = lax.optimization_barrier((both, left2, right2, *state))
    left6, right6 = shifted(left2, 4), shifted(right2, -4)
    grads = [both, *[turned(both, d) for d in range(1, n_y)]]
    state = absorb_stage(own, (left2, right2), ((0, 0),), ((1, 0),), queries, w_qkv, state)
    state = absorb_stage(
        own, (left_two, right_two), ((0, 1), (0, 0)), ((1, 0), (1, 1)), queries, w_qkv, state
    )
    attended, block_out = last_stage(
        own, (left6, right6), ((0, 0),), ((1, 0),), queries, w_qkv, state, frames, w_out
    )

    pieces = lax.all_to_all(attended, "y", 0, 0, tiled=True)
    share = grad_product(gathered_order(), pieces, core_swapped(pieces), grads)
    parts = lax.all_to_all(share.reshape(-1, WIDTH // N_SEQ, LANES), ("x", "z"), 0, 0, tiled=True)
    grad_scale = (lax.axis_size(("x", "core")) * N_SEQ * ROWS) ** (-0.5)
    return (block_out[None], jnp.sum(parts.astype(F32), axis=0) * grad_scale)


def solution(mesh):
    shape = (mesh.shape["dp"] // N_CORE, N_CORE, N_SEQ // N_Y, N_Y)
    chips = Mesh(mesh.devices.reshape(shape), ("x", "core", "z", "y"))
    groups = ("x", "core")
    placed = (P(groups, SEQ, None), P(groups, SEQ), P(), P(), P(), P(groups, SEQ, None))
    return jax.shard_map(
        local,
        mesh=chips,
        in_specs=placed,
        out_specs=(P(groups, SEQ, None), P(SEQ, groups)),
        check_vma=False,
    )
```

```python
import jax
import jax.numpy as jnp
from jax import lax
from jax.experimental import pallas as pl
from jax.experimental.pallas import tpu as pltpu
from jax.sharding import Mesh, PartitionSpec as P

ROWS = 128
LANES = 128
HALF = 64
WIDTH = 1024
CHUNKS = WIDTH // LANES
PACKED = WIDTH + 16
QUAD = 256
QUADS = WIDTH // QUAD
SEQ = ("z", "y")
NEG_BIG = -1e30
EPSILON = 1e-05
N_SEQ = 32
N_Y = 4
N_CORE = 2
LOG2E = 1.4426950408889634
AHEAD = 2
F32 = jnp.float32
BF16 = jnp.bfloat16
LIMIT = pltpu.CompilerParams(vmem_limit_bytes=40 * 1024 * 1024)


def shifted(block, distance):
    n_seq = lax.axis_size(SEQ)
    route = [(i, (i + distance) % n_seq) for i in range(n_seq)]
    return lax.ppermute(block, SEQ, route)


def core_swapped(block):
    return lax.ppermute(block, "core", [(0, 1), (1, 0)])


def turned(block, distance):
    n = lax.axis_size("y")
    return lax.ppermute(block, "y", [(i, (i + distance) % n) for i in range(n)])


def norm_kernel(core_ref, frames_hbm, ids_hbm, gain_hbm, cotangent_hbm, packed_ref, mine_ref, theirs_ref, *scratch):
    frames_ref, ids_ref, gain_ref, cotangent_ref, sems = scratch
    pairs = zip((frames_hbm, ids_hbm, gain_hbm, cotangent_hbm), scratch)
    copies = [pltpu.make_async_copy(src, dst, sems.at[i]) for i, (src, dst) in enumerate(pairs)]
    for copy in copies:
        copy.start()
    for copy in copies[:3]:
        copy.wait()
    float_frames = frames_ref[...].astype(F32)
    average = jnp.mean(float_frames, axis=-1, keepdims=True)
    centered = float_frames - average
    variance = jnp.mean(centered * centered, axis=-1, keepdims=True)
    normed = (centered * lax.rsqrt(variance + EPSILON) * gain_ref[...]).astype(BF16)
    for c in range(CHUNKS):
        packed_ref[c * ROWS : (c + 1) * ROWS, :] = normed[:, c * LANES : (c + 1) * LANES]
    ids = (ids_ref[...] + 1).astype(F32)
    packed_ref[WIDTH:PACKED, :] = jnp.broadcast_to(ids, (16, LANES)).astype(BF16)
    copies[3].wait()
    first = core_ref[0] == 0
    for c in range(CHUNKS // 2):
        even = cotangent_ref[:, 2 * c * LANES : (2 * c + 1) * LANES]
        odd = cotangent_ref[:, (2 * c + 1) * LANES : (2 * c + 2) * LANES]
        at = slice(c * LANES, (c + 1) * LANES)
        mine_ref[:, at] = jnp.where(first, even, odd)
        theirs_ref[:, at] = jnp.where(first, odd, even)


def normalize(core, frames, ids, gain, cotangent):
    hbm = pl.BlockSpec(memory_space=pltpu.HBM)
    half = jax.ShapeDtypeStruct((ROWS, WIDTH // 2), BF16)
    operands = (frames, ids, gain, cotangent)
    return pl.pallas_call(
        norm_kernel,
        in_specs=[pl.BlockSpec(memory_space=pltpu.SMEM)] + [hbm] * len(operands),
        out_shape=[jax.ShapeDtypeStruct((PACKED, LANES), BF16), half, half],
        scratch_shapes=[pltpu.VMEM(x.shape, x.dtype) for x in operands]
        + [pltpu.SemaphoreType.DMA((len(operands),))],
        compiler_params=pltpu.CompilerParams(vmem_limit_bytes=60 * 1024 * 1024),
        name="layer_norm",
    )(core, *operands)


def unpacked(block):
    ref, slot = block
    base = slot * PACKED
    chunks = [ref[base + c * ROWS : base + (c + 1) * ROWS, :] for c in range(CHUNKS)]
    return jnp.concatenate(chunks, axis=1)


def id_row(block):
    ref, slot = block
    base = slot * PACKED + WIDTH
    return ref[base : base + 16, :].astype(F32)[0:1, :]


def id_column(row):
    across = lax.broadcasted_iota(jnp.int32, (ROWS, LANES), 1)
    down = lax.broadcasted_iota(jnp.int32, (ROWS, LANES), 0)
    return jnp.sum(jnp.where(across == down, row, 0.0), axis=1, keepdims=True)


def projected(frames, weight_ref, section, quad):
    at = section * WIDTH + quad * QUAD
    block = weight_ref[:, at : at + QUAD]
    return jnp.dot(frames, block, preferred_element_type=F32).astype(BF16)


def absorb(frames, bias, queries_ref, weight_ref, state, first):
    tops_ref, sums_ref, acc_ref = state
    both = jnp.concatenate([bias, bias], axis=1)
    pairs = 2 * QUADS
    keys, flipped, waiting = {}, {}, []

    def score(index):
        quad, at = index // 2, (index % 2) * LANES
        if quad not in keys:
            keys[quad] = projected(frames, weight_ref, 1, quad)
            flipped[quad] = jnp.transpose(projected(frames, weight_ref, 2, quad))
        part = keys[quad][:, at : at + LANES]
        return jnp.dot(part, queries_ref[index], preferred_element_type=F32) + both

    for index in range(pairs + AHEAD):
        if index < pairs:
            waiting.append(score(index))
        if index < AHEAD:
            continue
        pair = index - AHEAD
        heads = (2 * pair, 2 * pair + 1)
        scores = waiting[pair]
        waiting[pair] = None
        top = jnp.max(scores, axis=0, keepdims=True)
        if not first:
            old_top = jnp.concatenate([tops_ref[h : h + 1, :] for h in heads], axis=1)
            old_sum = jnp.concatenate([sums_ref[h : h + 1, :] for h in heads], axis=1)
            top = jnp.maximum(old_top, top)
            rescale = jnp.exp2((old_top - top) * LOG2E)
        weights = jnp.exp2((scores - top) * LOG2E)
        total = jnp.sum(weights, axis=0, keepdims=True)
        at = (pair % 2) * LANES
        values = flipped[pair // 2][at : at + LANES, :]
        mixed = jnp.dot(values, weights.astype(BF16), preferred_element_type=F32)
        if not first:
            total = old_sum * rescale + total
        for k, h in enumerate(heads):
            lanes = slice(k * LANES, (k + 1) * LANES)
            rows = slice(h * HALF, (h + 1) * HALF)
            term = mixed[k * HALF : (k + 1) * HALF, lanes]
            if not first:
                term = acc_ref[rows, :] * rescale[:, lanes] + term
            acc_ref[rows, :] = term
            tops_ref[h : h + 1, :] = top[:, lanes]
            sums_ref[h : h + 1, :] = total[:, lanes]


def bias_of(blocks, own_row):
    columns = jnp.concatenate([id_column(id_row(block)) for block in blocks], axis=0)
    return jnp.where(columns == own_row, 0.0, NEG_BIG)


def own_kernel(own_ref, weight_ref, queries_ref, *state):
    frames = unpacked((own_ref, 0))
    row = id_row((own_ref, 0))
    for quad in range(QUADS):
        queries = projected(frames, weight_ref, 0, quad) * jnp.asarray(0.125, BF16)
        flipped = jnp.transpose(queries)
        zeros = jnp.zeros((HALF, ROWS), BF16)
        for pair in range(2):
            index = 2 * quad + pair
            at = pair * LANES
            queries_ref[index, 0:HALF, 0:ROWS] = flipped[at : at + HALF, :]
            queries_ref[index, 0:HALF, ROWS:] = zeros
            queries_ref[index, HALF:, 0:ROWS] = zeros
            queries_ref[index, HALF:, ROWS:] = flipped[at + HALF : at + LANES, :]
    absorb(frames, bias_of(((own_ref, 0),), row), queries_ref, weight_ref, state, True)


STATE_SHAPES = (
    jax.ShapeDtypeStruct((2 * CHUNKS, LANES), F32),
    jax.ShapeDtypeStruct((2 * CHUNKS, LANES), F32),
    jax.ShapeDtypeStruct((WIDTH, LANES), F32),
)


def cost(blocks, mib):
    return pl.CostEstimate(
        flops=2 * blocks * ROWS * WIDTH * 2 * WIDTH, bytes_accessed=mib << 20, transcendentals=0
    )


def own_block(own, w_qkv):
    return pl.pallas_call(
        own_kernel,
        out_shape=[jax.ShapeDtypeStruct((CHUNKS, LANES, 2 * ROWS), BF16), *STATE_SHAPES],
        compiler_params=LIMIT,
        cost_estimate=cost(3, 8),
        name="own_block",
    )(own, w_qkv)


def absorb_both(own_ref, left, right, queries_ref, weight_ref, state):
    own_row = id_row((own_ref, 0))
    left_needed = jnp.max(id_row(left[0])) == jnp.min(own_row)
    right_needed = jnp.min(id_row(right[0])) == jnp.max(own_row)

    @pl.when(left_needed | right_needed)
    def _():
        blocks = (*left, *right)
        frames = jnp.concatenate([unpacked(block) for block in blocks], axis=0)
        absorb(frames, bias_of(blocks, own_row), queries_ref, weight_ref, state, False)


def located(refs, places):
    return [(refs[i], slot) for i, slot in places]


def copied(old_state, state):
    for old, new in zip(old_state, state):
        new[...] = old[...]


def absorb_stage(own, blocks, left, right, queries, w_qkv, state):
    count = len(blocks)

    def kernel(own_ref, *refs):
        block_refs, refs = refs[:count], refs[count:]
        queries_ref, weight_ref = refs[:2]
        copied(refs[2:5], refs[5:8])
        absorb_both(
            own_ref, located(block_refs, left), located(block_refs, right), queries_ref, weight_ref, refs[5:8]
        )

    return pl.pallas_call(
        kernel,
        out_shape=list(STATE_SHAPES),
        compiler_params=LIMIT,
        cost_estimate=cost(len(left) + len(right), 8),
        name="absorb_stage",
    )(own, *blocks, queries, w_qkv, *state)


def last_stage(own, blocks, left, right, queries, w_qkv, state, frames, w_out):
    count = len(blocks)

    def kernel(own_ref, *refs):
        block_refs, refs = refs[:count], refs[count:]
        queries_ref, weight_ref = refs[:2]
        frames_ref, wout_ref, attended_ref, out_ref = refs[5:9]
        state_refs = refs[9:12]
        copied(refs[2:5], state_refs)
        absorb_both(
            own_ref, located(block_refs, left), located(block_refs, right), queries_ref, weight_ref, state_refs
        )
        _, sums_ref, acc_ref = state_refs
        n_y, rows = attended_ref.shape[0], WIDTH // N_SEQ
        chunks = []
        for c in range(CHUNKS):
            parts = []
            for h in (2 * c, 2 * c + 1):
                parts.append((acc_ref[h * HALF : (h + 1) * HALF, :] / sums_ref[h : h + 1, :]).astype(BF16))
            chunk = jnp.concatenate(parts, axis=0)
            for k in range(LANES // rows):
                z, y = divmod(c * (LANES // rows) + k, n_y)
                attended_ref[y, z * rows : (z + 1) * rows, :] = chunk[k * rows : (k + 1) * rows, :]
            chunks.append(jnp.transpose(chunk))
        attended = jnp.concatenate(chunks, axis=1)
        product = jnp.dot(attended, wout_ref[...], preferred_element_type=F32)
        out_ref[...] = (frames_ref[...].astype(F32) + product).astype(BF16)

    return pl.pallas_call(
        kernel,
        out_shape=[
            jax.ShapeDtypeStruct((N_Y, WIDTH // N_Y, LANES), BF16),
            jax.ShapeDtypeStruct((ROWS, WIDTH), BF16),
        ],
        scratch_shapes=[pltpu.VMEM(shape.shape, F32) for shape in STATE_SHAPES],
        compiler_params=LIMIT,
        cost_estimate=cost(len(left) + len(right) + 1, 10),
        name="last_stage",
    )(own, *blocks, queries, w_qkv, *state, frames, w_out)


def grad_kernel(place_ref, own_ref, other_ref, *refs):
    grads, out_ref = refs[:-1], refs[-1]
    count = len(grads)
    order = [lax.rem(place_ref[0] + count - i, count) for i in range(count)]
    attended = [ref[i] for i in order for ref in (own_ref, other_ref)]
    attended = jnp.concatenate(attended, axis=1)
    for half in range(2):
        at = slice(half * QUAD, (half + 1) * QUAD)
        block = jnp.concatenate([ref[:, at] for ref in grads], axis=0)
        product = jnp.dot(attended, block, preferred_element_type=F32).astype(BF16)
        for k in range(2):
            out_ref[2 * half + k] = product[:, k * LANES : (k + 1) * LANES]


def grad_product(place, own, other, grads):
    vmem = pl.BlockSpec(memory_space=pltpu.VMEM)
    rows, columns = own.shape[1], grads[0].shape[1]
    return pl.pallas_call(
        grad_kernel,
        in_specs=[pl.BlockSpec(memory_space=pltpu.SMEM)] + [vmem] * (2 + len(grads)),
        out_shape=jax.ShapeDtypeStruct((columns // LANES, rows, LANES), BF16),
        compiler_params=LIMIT,
        name="grad_product",
    )(place, own, other, *grads)


def local(frames, segment_ids, norm_gain, w_qkv, w_out, cotangent):
    n_y = lax.axis_size("y")
    frames = frames[0]
    core = lax.axis_index("core").astype(jnp.int32).reshape(1)
    place = lax.axis_index("y").astype(jnp.int32).reshape(1)
    own, mine, theirs = normalize(core, frames, segment_ids, norm_gain[None, :], cotangent[0])

    left1, right1 = shifted(own, 1), shifted(own, -1)
    left4, right4 = shifted(own, 4), shifted(own, -4)
    received = core_swapped(theirs)
    left2, right2 = shifted(left1, 1), shifted(right1, -1)
    left4, right4, near1, near2 = lax.optimization_barrier((left4, right4, left1, right1))
    near = jnp.concatenate([near1, near2], axis=0)
    left_two, right_two = shifted(near, 4), shifted(near, -4)
    held, near = lax.optimization_barrier((own, near))
    queries, *state = own_block(held, w_qkv)
    state = absorb_stage(
        own, (left1, left4, right1, right4), ((0, 0), (1, 0)), ((2, 0), (3, 0)), queries, w_qkv, state
    )
    both = jnp.concatenate([mine, received], axis=0)
    both, left2, right2, *state = lax.optimization_barrier((both, left2, right2, *state))
    left6, right6 = shifted(left2, 4), shifted(right2, -4)
    grads = [both, *[turned(both, d) for d in range(1, n_y)]]
    state = absorb_stage(own, (left2, right2), ((0, 0),), ((1, 0),), queries, w_qkv, state)
    state = absorb_stage(
        own, (left_two, right_two), ((0, 1), (0, 0)), ((1, 0), (1, 1)), queries, w_qkv, state
    )
    left6, right6, grads, state = lax.optimization_barrier((left6, right6, grads, state))
    attended, block_out = last_stage(
        own, (left6, right6), ((0, 0),), ((1, 0),), queries, w_qkv, state, frames, w_out
    )

    pieces = lax.all_to_all(attended, "y", 0, 0, tiled=True)
    share = grad_product(place, pieces, core_swapped(pieces), grads)
    parts = lax.all_to_all(share.reshape(-1, WIDTH // N_SEQ, LANES), ("x", "z"), 0, 0, tiled=True)
    grad_scale = (lax.axis_size(("x", "core")) * N_SEQ * ROWS) ** (-0.5)
    return (block_out[None], jnp.sum(parts.astype(F32), axis=0) * grad_scale)


def solution(mesh):
    shape = (mesh.shape["dp"] // N_CORE, N_CORE, N_SEQ // N_Y, N_Y)
    chips = Mesh(mesh.devices.reshape(shape), ("x", "core", "z", "y"))
    groups = ("x", "core")
    placed = (P(groups, SEQ, None), P(groups, SEQ), P(), P(), P(), P(groups, SEQ, None))
    return jax.shard_map(
        local,
        mesh=chips,
        in_specs=placed,
        out_specs=(P(groups, SEQ, None), P(SEQ, groups)),
        check_vma=False,
    )
```

```python
import jax
import jax.numpy as jnp
from jax import lax
from jax.experimental import pallas as pl
from jax.experimental.pallas import tpu as pltpu
from jax.sharding import Mesh, PartitionSpec as P

ROWS = 128
LANES = 128
HALF = 64
WIDTH = 1024
CHUNKS = WIDTH // LANES
PACKED = WIDTH + 16
QUAD = 256
QUADS = WIDTH // QUAD
SEQ = ("z", "y")
NEG_BIG = -1e30
EPSILON = 1e-05
N_SEQ = 32
N_Y = 4
N_CORE = 2
LOG2E = 1.4426950408889634
AHEAD = 2
F32 = jnp.float32
BF16 = jnp.bfloat16
LIMIT = pltpu.CompilerParams(vmem_limit_bytes=40 * 1024 * 1024)


def shifted(block, distance):
    n_seq = lax.axis_size(SEQ)
    route = [(i, (i + distance) % n_seq) for i in range(n_seq)]
    return lax.ppermute(block, SEQ, route)


def core_swapped(block):
    return lax.ppermute(block, "core", [(0, 1), (1, 0)])


def turned(block, distance):
    n = lax.axis_size("y")
    return lax.ppermute(block, "y", [(i, (i + distance) % n) for i in range(n)])


def norm_kernel(frames_hbm, ids_hbm, gain_hbm, packed_ref, frames_ref, ids_ref, gain_ref, sems):
    pairs = ((frames_hbm, frames_ref), (ids_hbm, ids_ref), (gain_hbm, gain_ref))
    copies = [pltpu.make_async_copy(src, dst, sems.at[i]) for i, (src, dst) in enumerate(pairs)]
    for copy in copies:
        copy.start()
    for copy in copies:
        copy.wait()
    float_frames = frames_ref[...].astype(F32)
    average = jnp.mean(float_frames, axis=-1, keepdims=True)
    centered = float_frames - average
    variance = jnp.mean(centered * centered, axis=-1, keepdims=True)
    normed = (centered * lax.rsqrt(variance + EPSILON) * gain_ref[...]).astype(BF16)
    for c in range(CHUNKS):
        packed_ref[c * ROWS : (c + 1) * ROWS, :] = normed[:, c * LANES : (c + 1) * LANES]
    ids = (ids_ref[...] + 1).astype(F32)
    packed_ref[WIDTH:PACKED, :] = jnp.broadcast_to(ids, (16, LANES)).astype(BF16)


def normalize(*operands):
    hbm = pl.BlockSpec(memory_space=pltpu.HBM)
    return pl.pallas_call(
        norm_kernel,
        in_specs=[hbm] * len(operands),
        out_shape=jax.ShapeDtypeStruct((PACKED, LANES), BF16),
        scratch_shapes=[pltpu.VMEM(x.shape, x.dtype) for x in operands]
        + [pltpu.SemaphoreType.DMA((len(operands),))],
        compiler_params=pltpu.CompilerParams(vmem_limit_bytes=60 * 1024 * 1024),
        name="layer_norm",
    )(*operands)


def split_kernel(core_ref, cotangent_ref, mine_ref, theirs_ref):
    first = core_ref[0] == 0
    for c in range(CHUNKS // 2):
        even = cotangent_ref[:, 2 * c * LANES : (2 * c + 1) * LANES]
        odd = cotangent_ref[:, (2 * c + 1) * LANES : (2 * c + 2) * LANES]
        at = slice(c * LANES, (c + 1) * LANES)
        mine_ref[:, at] = jnp.where(first, even, odd)
        theirs_ref[:, at] = jnp.where(first, odd, even)


def split_columns(core, cotangent):
    half = jax.ShapeDtypeStruct((ROWS, WIDTH // 2), BF16)
    return pl.pallas_call(
        split_kernel,
        in_specs=[pl.BlockSpec(memory_space=pltpu.SMEM), pl.BlockSpec(memory_space=pltpu.VMEM)],
        out_shape=[half, half],
        compiler_params=LIMIT,
        name="split_columns",
    )(core, cotangent)


def unpacked(block):
    ref, slot = block
    base = slot * PACKED
    chunks = [ref[base + c * ROWS : base + (c + 1) * ROWS, :] for c in range(CHUNKS)]
    return jnp.concatenate(chunks, axis=1)


def id_row(block):
    ref, slot = block
    base = slot * PACKED + WIDTH
    return ref[base : base + 16, :].astype(F32)[0:1, :]


def id_column(row):
    across = lax.broadcasted_iota(jnp.int32, (ROWS, LANES), 1)
    down = lax.broadcasted_iota(jnp.int32, (ROWS, LANES), 0)
    return jnp.sum(jnp.where(across == down, row, 0.0), axis=1, keepdims=True)


def projected(frames, weight_ref, section, quad):
    at = section * WIDTH + quad * QUAD
    block = weight_ref[:, at : at + QUAD]
    return jnp.dot(frames, block, preferred_element_type=F32).astype(BF16)


def absorb(frames, bias, queries_ref, weight_ref, state, first):
    tops_ref, sums_ref, acc_ref = state
    both = jnp.concatenate([bias, bias], axis=1)
    pairs = 2 * QUADS
    keys, flipped, waiting = {}, {}, []

    def score(index):
        quad, at = index // 2, (index % 2) * LANES
        if quad not in keys:
            keys[quad] = projected(frames, weight_ref, 1, quad)
            flipped[quad] = jnp.transpose(projected(frames, weight_ref, 2, quad))
        part = keys[quad][:, at : at + LANES]
        return jnp.dot(part, queries_ref[index], preferred_element_type=F32) + both

    for index in range(pairs + AHEAD):
        if index < pairs:
            waiting.append(score(index))
        if index < AHEAD:
            continue
        pair = index - AHEAD
        heads = (2 * pair, 2 * pair + 1)
        scores = waiting[pair]
        waiting[pair] = None
        top = jnp.max(scores, axis=0, keepdims=True)
        if not first:
            old_top = jnp.concatenate([tops_ref[h : h + 1, :] for h in heads], axis=1)
            old_sum = jnp.concatenate([sums_ref[h : h + 1, :] for h in heads], axis=1)
            top = jnp.maximum(old_top, top)
            rescale = jnp.exp2((old_top - top) * LOG2E)
        weights = jnp.exp2((scores - top) * LOG2E)
        total = jnp.sum(weights, axis=0, keepdims=True)
        at = (pair % 2) * LANES
        values = flipped[pair // 2][at : at + LANES, :]
        mixed = jnp.dot(values, weights.astype(BF16), preferred_element_type=F32)
        if not first:
            total = old_sum * rescale + total
        for k, h in enumerate(heads):
            lanes = slice(k * LANES, (k + 1) * LANES)
            rows = slice(h * HALF, (h + 1) * HALF)
            term = mixed[k * HALF : (k + 1) * HALF, lanes]
            if not first:
                term = acc_ref[rows, :] * rescale[:, lanes] + term
            acc_ref[rows, :] = term
            tops_ref[h : h + 1, :] = top[:, lanes]
            sums_ref[h : h + 1, :] = total[:, lanes]


def bias_of(blocks, own_row):
    columns = jnp.concatenate([id_column(id_row(block)) for block in blocks], axis=0)
    return jnp.where(columns == own_row, 0.0, NEG_BIG)


def own_kernel(own_ref, weight_ref, queries_ref, *state):
    frames = unpacked((own_ref, 0))
    row = id_row((own_ref, 0))
    for quad in range(QUADS):
        queries = projected(frames, weight_ref, 0, quad) * jnp.asarray(0.125, BF16)
        flipped = jnp.transpose(queries)
        zeros = jnp.zeros((HALF, ROWS), BF16)
        for pair in range(2):
            index = 2 * quad + pair
            at = pair * LANES
            queries_ref[index, 0:HALF, 0:ROWS] = flipped[at : at + HALF, :]
            queries_ref[index, 0:HALF, ROWS:] = zeros
            queries_ref[index, HALF:, 0:ROWS] = zeros
            queries_ref[index, HALF:, ROWS:] = flipped[at + HALF : at + LANES, :]
    absorb(frames, bias_of(((own_ref, 0),), row), queries_ref, weight_ref, state, True)


STATE_SHAPES = (
    jax.ShapeDtypeStruct((2 * CHUNKS, LANES), F32),
    jax.ShapeDtypeStruct((2 * CHUNKS, LANES), F32),
    jax.ShapeDtypeStruct((WIDTH, LANES), F32),
)


def cost(blocks, mib):
    return pl.CostEstimate(
        flops=2 * blocks * ROWS * WIDTH * 2 * WIDTH, bytes_accessed=mib << 20, transcendentals=0
    )


def own_block(own, w_qkv):
    return pl.pallas_call(
        own_kernel,
        out_shape=[jax.ShapeDtypeStruct((CHUNKS, LANES, 2 * ROWS), BF16), *STATE_SHAPES],
        compiler_params=LIMIT,
        cost_estimate=cost(3, 8),
        name="own_block",
    )(own, w_qkv)


def absorb_both(own_ref, left, right, queries_ref, weight_ref, state):
    own_row = id_row((own_ref, 0))
    left_needed = jnp.max(id_row(left[0])) == jnp.min(own_row)
    right_needed = jnp.min(id_row(right[0])) == jnp.max(own_row)

    @pl.when(left_needed | right_needed)
    def _():
        blocks = (*left, *right)
        frames = jnp.concatenate([unpacked(block) for block in blocks], axis=0)
        absorb(frames, bias_of(blocks, own_row), queries_ref, weight_ref, state, False)


def located(refs, places):
    return [(refs[i], slot) for i, slot in places]


def copied(old_state, state):
    for old, new in zip(old_state, state):
        new[...] = old[...]


def absorb_stage(own, blocks, left, right, queries, w_qkv, state):
    count = len(blocks)

    def kernel(own_ref, *refs):
        block_refs, refs = refs[:count], refs[count:]
        queries_ref, weight_ref = refs[:2]
        copied(refs[2:5], refs[5:8])
        absorb_both(
            own_ref, located(block_refs, left), located(block_refs, right), queries_ref, weight_ref, refs[5:8]
        )

    return pl.pallas_call(
        kernel,
        out_shape=list(STATE_SHAPES),
        compiler_params=LIMIT,
        cost_estimate=cost(len(left) + len(right), 8),
        name="absorb_stage",
    )(own, *blocks, queries, w_qkv, *state)


def last_stage(own, blocks, left, right, queries, w_qkv, state, frames, w_out):
    count = len(blocks)

    def kernel(own_ref, *refs):
        block_refs, refs = refs[:count], refs[count:]
        queries_ref, weight_ref = refs[:2]
        frames_ref, wout_ref, attended_ref, out_ref = refs[5:9]
        state_refs = refs[9:12]
        copied(refs[2:5], state_refs)
        absorb_both(
            own_ref, located(block_refs, left), located(block_refs, right), queries_ref, weight_ref, state_refs
        )
        _, sums_ref, acc_ref = state_refs
        n_y, rows = attended_ref.shape[0], WIDTH // N_SEQ
        chunks = []
        for c in range(CHUNKS):
            parts = []
            for h in (2 * c, 2 * c + 1):
                parts.append((acc_ref[h * HALF : (h + 1) * HALF, :] / sums_ref[h : h + 1, :]).astype(BF16))
            chunk = jnp.concatenate(parts, axis=0)
            for k in range(LANES // rows):
                z, y = divmod(c * (LANES // rows) + k, n_y)
                attended_ref[y, z * rows : (z + 1) * rows, :] = chunk[k * rows : (k + 1) * rows, :]
            chunks.append(jnp.transpose(chunk))
        attended = jnp.concatenate(chunks, axis=1)
        product = jnp.dot(attended, wout_ref[...], preferred_element_type=F32)
        out_ref[...] = (frames_ref[...].astype(F32) + product).astype(BF16)

    return pl.pallas_call(
        kernel,
        out_shape=[
            jax.ShapeDtypeStruct((N_Y, WIDTH // N_Y, LANES), BF16),
            jax.ShapeDtypeStruct((ROWS, WIDTH), BF16),
        ],
        scratch_shapes=[pltpu.VMEM(shape.shape, F32) for shape in STATE_SHAPES],
        compiler_params=LIMIT,
        cost_estimate=cost(len(left) + len(right) + 1, 10),
        name="last_stage",
    )(own, *blocks, queries, w_qkv, *state, frames, w_out)


def grad_kernel(place_ref, own_ref, other_ref, *refs):
    grads, out_ref = refs[:-1], refs[-1]
    count = len(grads)
    order = [lax.rem(place_ref[0] + count - i, count) for i in range(count)]
    attended = [ref[i] for i in order for ref in (own_ref, other_ref)]
    attended = jnp.concatenate(attended, axis=1)
    for half in range(2):
        at = slice(half * QUAD, (half + 1) * QUAD)
        block = jnp.concatenate([ref[:, at] for ref in grads], axis=0)
        product = jnp.dot(attended, block, preferred_element_type=F32).astype(BF16)
        for k in range(2):
            out_ref[2 * half + k] = product[:, k * LANES : (k + 1) * LANES]


def grad_product(place, own, other, grads):
    vmem = pl.BlockSpec(memory_space=pltpu.VMEM)
    rows, columns = own.shape[1], grads[0].shape[1]
    return pl.pallas_call(
        grad_kernel,
        in_specs=[pl.BlockSpec(memory_space=pltpu.SMEM)] + [vmem] * (2 + len(grads)),
        out_shape=jax.ShapeDtypeStruct((columns // LANES, rows, LANES), BF16),
        compiler_params=LIMIT,
        name="grad_product",
    )(place, own, other, *grads)


def local(frames, segment_ids, norm_gain, w_qkv, w_out, cotangent):
    n_y = lax.axis_size("y")
    frames = frames[0]
    core = lax.axis_index("core").astype(jnp.int32).reshape(1)
    place = lax.axis_index("y").astype(jnp.int32).reshape(1)
    own = normalize(frames, segment_ids, norm_gain[None, :])

    left1, right1 = shifted(own, 1), shifted(own, -1)
    left2, right2 = shifted(own, 2), shifted(own, -2)
    queries, *state = own_block(own, w_qkv)
    left1, right1, queries = lax.optimization_barrier((left1, right1, queries))
    trio = jnp.concatenate([left1, own, right1], axis=0)
    left_trio, right_trio = shifted(trio, 4), shifted(trio, -4)
    trio, cotangent = lax.optimization_barrier((trio, cotangent))
    mine, theirs = split_columns(core, cotangent[0])
    received = core_swapped(theirs)
    state = absorb_stage(own, (left1, right1), ((0, 0),), ((1, 0),), queries, w_qkv, state)
    both = jnp.concatenate([mine, received], axis=0)
    both, left2, right2, *state = lax.optimization_barrier((both, left2, right2, *state))
    left6, right6 = shifted(left2, 4), shifted(right2, -4)
    state = absorb_stage(own, (left2, right2), ((0, 0),), ((1, 0),), queries, w_qkv, state)
    both, *state = lax.optimization_barrier((both, *state))
    grads = [both, *[turned(both, d) for d in range(1, n_y)]]
    state = absorb_stage(
        own, (left_trio, right_trio), ((0, 2), (0, 1), (0, 0)), ((1, 0), (1, 1), (1, 2)),
        queries, w_qkv, state,
    )
    left6, right6, grads, state = lax.optimization_barrier((left6, right6, grads, state))
    attended, block_out = last_stage(
        own, (left6, right6), ((0, 0),), ((1, 0),), queries, w_qkv, state, frames, w_out
    )

    pieces = lax.all_to_all(attended, "y", 0, 0, tiled=True)
    share = grad_product(place, pieces, core_swapped(pieces), grads)
    parts = lax.all_to_all(share.reshape(-1, WIDTH // N_SEQ, LANES), ("x", "z"), 0, 0, tiled=True)
    grad_scale = (lax.axis_size(("x", "core")) * N_SEQ * ROWS) ** (-0.5)
    return (block_out[None], jnp.sum(parts.astype(F32), axis=0) * grad_scale)


def solution(mesh):
    shape = (mesh.shape["dp"] // N_CORE, N_CORE, N_SEQ // N_Y, N_Y)
    chips = Mesh(mesh.devices.reshape(shape), ("x", "core", "z", "y"))
    groups = ("x", "core")
    placed = (P(groups, SEQ, None), P(groups, SEQ), P(), P(), P(), P(groups, SEQ, None))
    return jax.shard_map(
        local,
        mesh=chips,
        in_specs=placed,
        out_specs=(P(groups, SEQ, None), P(SEQ, groups)),
        check_vma=False,
    )
```

```python
import jax
import jax.numpy as jnp
from jax import lax
from jax.experimental import pallas as pl
from jax.experimental.pallas import tpu as pltpu
from jax.sharding import Mesh, PartitionSpec as P

ROWS = 128
LANES = 128
HALF = 64
WIDTH = 1024
CHUNKS = WIDTH // LANES
PACKED = WIDTH + 16
QUAD = 256
QUADS = WIDTH // QUAD
SEQ = ("z", "y")
NEG_BIG = -1e30
EPSILON = 1e-05
N_SEQ = 32
N_Y = 4
N_CORE = 2
LOG2E = 1.4426950408889634
AHEAD = 2
F32 = jnp.float32
BF16 = jnp.bfloat16
LIMIT = pltpu.CompilerParams(vmem_limit_bytes=24 * 1024 * 1024)


def shifted(block, distance):
    n_seq = lax.axis_size(SEQ)
    route = [(i, (i + distance) % n_seq) for i in range(n_seq)]
    return lax.ppermute(block, SEQ, route)


def core_swapped(block):
    return lax.ppermute(block, "core", [(0, 1), (1, 0)])


def turned(block, distance):
    n = lax.axis_size("y")
    return lax.ppermute(block, "y", [(i, (i + distance) % n) for i in range(n)])


def norm_kernel(core_ref, frames_hbm, ids_hbm, gain_hbm, cotangent_hbm, packed_ref, mine_ref, theirs_ref, *scratch):
    frames_ref, ids_ref, gain_ref, cotangent_ref, sems = scratch
    pairs = zip((frames_hbm, ids_hbm, gain_hbm, cotangent_hbm), scratch)
    copies = [pltpu.make_async_copy(src, dst, sems.at[i]) for i, (src, dst) in enumerate(pairs)]
    for copy in copies:
        copy.start()
    for copy in copies[:3]:
        copy.wait()
    float_frames = frames_ref[...].astype(F32)
    average = jnp.mean(float_frames, axis=-1, keepdims=True)
    centered = float_frames - average
    variance = jnp.mean(centered * centered, axis=-1, keepdims=True)
    normed = (centered * lax.rsqrt(variance + EPSILON) * gain_ref[...]).astype(BF16)
    for c in range(CHUNKS):
        packed_ref[c * ROWS : (c + 1) * ROWS, :] = normed[:, c * LANES : (c + 1) * LANES]
    ids = (ids_ref[...] + 1).astype(F32)
    packed_ref[WIDTH:PACKED, :] = jnp.broadcast_to(ids, (16, LANES)).astype(BF16)
    copies[3].wait()
    first = core_ref[0] == 0
    for c in range(CHUNKS // 2):
        even = cotangent_ref[:, 2 * c * LANES : (2 * c + 1) * LANES]
        odd = cotangent_ref[:, (2 * c + 1) * LANES : (2 * c + 2) * LANES]
        at = slice(c * LANES, (c + 1) * LANES)
        mine_ref[:, at] = jnp.where(first, even, odd)
        theirs_ref[:, at] = jnp.where(first, odd, even)


def normalize(core, frames, ids, gain, cotangent):
    hbm = pl.BlockSpec(memory_space=pltpu.HBM)
    half = jax.ShapeDtypeStruct((ROWS, WIDTH // 2), BF16)
    operands = (frames, ids, gain, cotangent)
    return pl.pallas_call(
        norm_kernel,
        in_specs=[pl.BlockSpec(memory_space=pltpu.SMEM)] + [hbm] * len(operands),
        out_shape=[jax.ShapeDtypeStruct((PACKED, LANES), BF16), half, half],
        scratch_shapes=[pltpu.VMEM(x.shape, x.dtype) for x in operands]
        + [pltpu.SemaphoreType.DMA((len(operands),))],
        compiler_params=pltpu.CompilerParams(vmem_limit_bytes=60 * 1024 * 1024),
        name="layer_norm",
    )(core, *operands)


def unpacked(block):
    ref, slot = block
    base = slot * PACKED
    chunks = [ref[base + c * ROWS : base + (c + 1) * ROWS, :] for c in range(CHUNKS)]
    return jnp.concatenate(chunks, axis=1)


def id_row(block):
    ref, slot = block
    base = slot * PACKED + WIDTH
    return ref[base : base + 16, :].astype(F32)[0:1, :]


def id_column(row):
    across = lax.broadcasted_iota(jnp.int32, (ROWS, LANES), 1)
    down = lax.broadcasted_iota(jnp.int32, (ROWS, LANES), 0)
    return jnp.sum(jnp.where(across == down, row, 0.0), axis=1, keepdims=True)


def projected(frames, weight_ref, section, quad):
    at = section * WIDTH + quad * QUAD
    block = weight_ref[:, at : at + QUAD]
    return jnp.dot(frames, block, preferred_element_type=F32).astype(BF16)


def absorb(frames, bias, queries_ref, weight_ref, state, first):
    tops_ref, sums_ref, acc_ref = state
    both = jnp.concatenate([bias, bias], axis=1)
    pairs = 2 * QUADS
    keys, flipped, waiting = {}, {}, []

    def score(index):
        quad, at = index // 2, (index % 2) * LANES
        if quad not in keys:
            keys[quad] = projected(frames, weight_ref, 1, quad)
            flipped[quad] = jnp.transpose(projected(frames, weight_ref, 2, quad))
        part = keys[quad][:, at : at + LANES]
        return jnp.dot(part, queries_ref[index], preferred_element_type=F32) + both

    for index in range(pairs + AHEAD):
        if index < pairs:
            waiting.append(score(index))
        if index < AHEAD:
            continue
        pair = index - AHEAD
        heads = (2 * pair, 2 * pair + 1)
        scores = waiting[pair]
        waiting[pair] = None
        top = jnp.max(scores, axis=0, keepdims=True)
        if not first:
            old_top = jnp.concatenate([tops_ref[h : h + 1, :] for h in heads], axis=1)
            old_sum = jnp.concatenate([sums_ref[h : h + 1, :] for h in heads], axis=1)
            top = jnp.maximum(old_top, top)
            rescale = jnp.exp2((old_top - top) * LOG2E)
        weights = jnp.exp2((scores - top) * LOG2E)
        total = jnp.sum(weights, axis=0, keepdims=True)
        at = (pair % 2) * LANES
        values = flipped[pair // 2][at : at + LANES, :]
        mixed = jnp.dot(values, weights.astype(BF16), preferred_element_type=F32)
        if not first:
            total = old_sum * rescale + total
        for k, h in enumerate(heads):
            lanes = slice(k * LANES, (k + 1) * LANES)
            rows = slice(h * HALF, (h + 1) * HALF)
            term = mixed[k * HALF : (k + 1) * HALF, lanes]
            if not first:
                term = acc_ref[rows, :] * rescale[:, lanes] + term
            acc_ref[rows, :] = term
            tops_ref[h : h + 1, :] = top[:, lanes]
            sums_ref[h : h + 1, :] = total[:, lanes]


def bias_of(blocks, own_row):
    columns = jnp.concatenate([id_column(id_row(block)) for block in blocks], axis=0)
    return jnp.where(columns == own_row, 0.0, NEG_BIG)


def own_kernel(own_ref, weight_ref, queries_ref, *state):
    frames = unpacked((own_ref, 0))
    row = id_row((own_ref, 0))
    for quad in range(QUADS):
        queries = projected(frames, weight_ref, 0, quad) * jnp.asarray(0.125, BF16)
        flipped = jnp.transpose(queries)
        zeros = jnp.zeros((HALF, ROWS), BF16)
        for pair in range(2):
            index = 2 * quad + pair
            at = pair * LANES
            queries_ref[index, 0:HALF, 0:ROWS] = flipped[at : at + HALF, :]
            queries_ref[index, 0:HALF, ROWS:] = zeros
            queries_ref[index, HALF:, 0:ROWS] = zeros
            queries_ref[index, HALF:, ROWS:] = flipped[at + HALF : at + LANES, :]
    absorb(frames, bias_of(((own_ref, 0),), row), queries_ref, weight_ref, state, True)


STATE_SHAPES = (
    jax.ShapeDtypeStruct((2 * CHUNKS, LANES), F32),
    jax.ShapeDtypeStruct((2 * CHUNKS, LANES), F32),
    jax.ShapeDtypeStruct((WIDTH, LANES), F32),
)


def cost(blocks, mib):
    return pl.CostEstimate(
        flops=2 * blocks * ROWS * WIDTH * 2 * WIDTH, bytes_accessed=mib << 20, transcendentals=0
    )


def own_block(own, w_qkv):
    return pl.pallas_call(
        own_kernel,
        out_shape=[jax.ShapeDtypeStruct((CHUNKS, LANES, 2 * ROWS), BF16), *STATE_SHAPES],
        compiler_params=LIMIT,
        cost_estimate=cost(3, 8),
        name="own_block",
    )(own, w_qkv)


def absorb_both(own_ref, left, right, queries_ref, weight_ref, state):
    own_row = id_row((own_ref, 0))
    left_needed = jnp.max(id_row(left[0])) == jnp.min(own_row)
    right_needed = jnp.min(id_row(right[0])) == jnp.max(own_row)

    @pl.when(left_needed | right_needed)
    def _():
        blocks = (*left, *right)
        frames = jnp.concatenate([unpacked(block) for block in blocks], axis=0)
        absorb(frames, bias_of(blocks, own_row), queries_ref, weight_ref, state, False)


def located(refs, places):
    return [(refs[i], slot) for i, slot in places]


def copied(old_state, state):
    for old, new in zip(old_state, state):
        new[...] = old[...]


def absorb_stage(own, blocks, left, right, queries, w_qkv, state):
    count = len(blocks)

    def kernel(own_ref, *refs):
        block_refs, refs = refs[:count], refs[count:]
        queries_ref, weight_ref = refs[:2]
        copied(refs[2:5], refs[5:8])
        absorb_both(
            own_ref, located(block_refs, left), located(block_refs, right), queries_ref, weight_ref, refs[5:8]
        )

    return pl.pallas_call(
        kernel,
        out_shape=list(STATE_SHAPES),
        compiler_params=LIMIT,
        cost_estimate=cost(len(left) + len(right), 8),
        name="absorb_stage",
    )(own, *blocks, queries, w_qkv, *state)


def last_stage(own, blocks, left, right, queries, w_qkv, state, frames, w_out):
    count = len(blocks)

    def kernel(own_ref, *refs):
        block_refs, refs = refs[:count], refs[count:]
        queries_ref, weight_ref = refs[:2]
        frames_ref, wout_ref, attended_ref, out_ref = refs[5:9]
        state_refs = refs[9:12]
        copied(refs[2:5], state_refs)
        absorb_both(
            own_ref, located(block_refs, left), located(block_refs, right), queries_ref, weight_ref, state_refs
        )
        _, sums_ref, acc_ref = state_refs
        n_y, rows = attended_ref.shape[0], WIDTH // N_SEQ
        chunks = []
        for c in range(CHUNKS):
            parts = []
            for h in (2 * c, 2 * c + 1):
                parts.append((acc_ref[h * HALF : (h + 1) * HALF, :] / sums_ref[h : h + 1, :]).astype(BF16))
            chunk = jnp.concatenate(parts, axis=0)
            for k in range(LANES // rows):
                z, y = divmod(c * (LANES // rows) + k, n_y)
                attended_ref[y, z * rows : (z + 1) * rows, :] = chunk[k * rows : (k + 1) * rows, :]
            chunks.append(jnp.transpose(chunk))
        attended = jnp.concatenate(chunks, axis=1)
        product = jnp.dot(attended, wout_ref[...], preferred_element_type=F32)
        out_ref[...] = (frames_ref[...].astype(F32) + product).astype(BF16)

    return pl.pallas_call(
        kernel,
        out_shape=[
            jax.ShapeDtypeStruct((N_Y, WIDTH // N_Y, LANES), BF16),
            jax.ShapeDtypeStruct((ROWS, WIDTH), BF16),
        ],
        scratch_shapes=[pltpu.VMEM(shape.shape, F32) for shape in STATE_SHAPES],
        compiler_params=LIMIT,
        cost_estimate=cost(len(left) + len(right) + 1, 10),
        name="last_stage",
    )(own, *blocks, queries, w_qkv, *state, frames, w_out)


def grad_kernel(place_ref, own_ref, other_ref, *refs):
    grads, out_ref = refs[:-1], refs[-1]
    count = len(grads)
    order = [lax.rem(place_ref[0] + count - i, count) for i in range(count)]
    attended = [ref[i] for i in order for ref in (own_ref, other_ref)]
    attended = jnp.concatenate(attended, axis=1)
    for half in range(2):
        at = slice(half * QUAD, (half + 1) * QUAD)
        block = jnp.concatenate([ref[:, at] for ref in grads], axis=0)
        product = jnp.dot(attended, block, preferred_element_type=F32).astype(BF16)
        for k in range(2):
            out_ref[2 * half + k] = product[:, k * LANES : (k + 1) * LANES]


def grad_product(place, own, other, grads):
    vmem = pl.BlockSpec(memory_space=pltpu.VMEM)
    rows, columns = own.shape[1], grads[0].shape[1]
    return pl.pallas_call(
        grad_kernel,
        in_specs=[pl.BlockSpec(memory_space=pltpu.SMEM)] + [vmem] * (2 + len(grads)),
        out_shape=jax.ShapeDtypeStruct((columns // LANES, rows, LANES), BF16),
        compiler_params=LIMIT,
        name="grad_product",
    )(place, own, other, *grads)


def local(frames, segment_ids, norm_gain, w_qkv, w_out, cotangent):
    n_y = lax.axis_size("y")
    frames = frames[0]
    core = lax.axis_index("core").astype(jnp.int32).reshape(1)
    place = lax.axis_index("y").astype(jnp.int32).reshape(1)
    own, mine, theirs = normalize(core, frames, segment_ids, norm_gain[None, :], cotangent[0])

    left1, right1 = shifted(own, 1), shifted(own, -1)
    left4, right4 = shifted(own, 4), shifted(own, -4)
    received = core_swapped(theirs)
    queries, *state = own_block(own, w_qkv)
    left1, right1, queries = lax.optimization_barrier((left1, right1, queries))
    near = jnp.concatenate([left1, right1], axis=0)
    left_two, right_two = shifted(near, 4), shifted(near, -4)
    state = absorb_stage(
        own, (left1, left4, right1, right4), ((0, 0), (1, 0)), ((2, 0), (3, 0)), queries, w_qkv, state
    )
    both = jnp.concatenate([mine, received], axis=0)
    both, near1, near2, *state = lax.optimization_barrier((both, left1, right1, *state))
    left2, right2 = shifted(near1, 1), shifted(near2, -1)
    grads = [both, *[turned(both, d) for d in range(1, n_y)]]
    state = absorb_stage(own, (left2, right2), ((0, 0),), ((1, 0),), queries, w_qkv, state)
    left6, right6 = shifted(left_two[:PACKED], 1), shifted(right_two[PACKED:], -1)
    state = absorb_stage(
        own, (left_two, right_two), ((0, 1), (0, 0)), ((1, 0), (1, 1)), queries, w_qkv, state
    )
    left6, right6, grads, state = lax.optimization_barrier((left6, right6, grads, state))
    attended, block_out = last_stage(
        own, (left6, right6), ((0, 0),), ((1, 0),), queries, w_qkv, state, frames, w_out
    )

    pieces = lax.all_to_all(attended, "y", 0, 0, tiled=True)
    share = grad_product(place, pieces, core_swapped(pieces), grads)
    parts = lax.all_to_all(share.reshape(-1, WIDTH // N_SEQ, LANES), ("x", "z"), 0, 0, tiled=True)
    grad_scale = (lax.axis_size(("x", "core")) * N_SEQ * ROWS) ** (-0.5)
    return (block_out[None], jnp.sum(parts.astype(F32), axis=0) * grad_scale)


def solution(mesh):
    shape = (mesh.shape["dp"] // N_CORE, N_CORE, N_SEQ // N_Y, N_Y)
    chips = Mesh(mesh.devices.reshape(shape), ("x", "core", "z", "y"))
    groups = ("x", "core")
    placed = (P(groups, SEQ, None), P(groups, SEQ), P(), P(), P(), P(groups, SEQ, None))
    return jax.shard_map(
        local,
        mesh=chips,
        in_specs=placed,
        out_specs=(P(groups, SEQ, None), P(SEQ, groups)),
        check_vma=False,
    )
```

```python
import jax
import jax.numpy as jnp
from jax import lax
from jax.experimental import pallas as pl
from jax.experimental.pallas import tpu as pltpu
from jax.sharding import Mesh, PartitionSpec as P

ROWS = 128
LANES = 128
HALF = 64
WIDTH = 1024
CHUNKS = WIDTH // LANES
PACKED = WIDTH + 16
QUAD = 256
QUADS = WIDTH // QUAD
SEQ = ("z", "y")
NEG_BIG = -1e30
EPSILON = 1e-05
N_SEQ = 32
N_Y = 4
N_CORE = 2
LOG2E = 1.4426950408889634
AHEAD = 2
F32 = jnp.float32
BF16 = jnp.bfloat16
LIMIT = pltpu.CompilerParams(vmem_limit_bytes=24 * 1024 * 1024)


def shifted(block, distance):
    n_seq = lax.axis_size(SEQ)
    route = [(i, (i + distance) % n_seq) for i in range(n_seq)]
    return lax.ppermute(block, SEQ, route)


def core_swapped(block):
    return lax.ppermute(block, "core", [(0, 1), (1, 0)])


def turned(block, distance):
    n = lax.axis_size("y")
    return lax.ppermute(block, "y", [(i, (i + distance) % n) for i in range(n)])


def norm_kernel(core_ref, frames_hbm, ids_hbm, gain_hbm, cotangent_hbm, packed_ref, mine_ref, theirs_ref, *scratch):
    frames_ref, ids_ref, gain_ref, cotangent_ref, sems = scratch
    pairs = zip((frames_hbm, ids_hbm, gain_hbm, cotangent_hbm), scratch)
    copies = [pltpu.make_async_copy(src, dst, sems.at[i]) for i, (src, dst) in enumerate(pairs)]
    for copy in copies:
        copy.start()
    for copy in copies[:3]:
        copy.wait()
    float_frames = frames_ref[...].astype(F32)
    average = jnp.mean(float_frames, axis=-1, keepdims=True)
    centered = float_frames - average
    variance = jnp.mean(centered * centered, axis=-1, keepdims=True)
    normed = (centered * lax.rsqrt(variance + EPSILON) * gain_ref[...]).astype(BF16)
    for c in range(CHUNKS):
        packed_ref[c * ROWS : (c + 1) * ROWS, :] = normed[:, c * LANES : (c + 1) * LANES]
    ids = (ids_ref[...] + 1).astype(F32)
    packed_ref[WIDTH:PACKED, :] = jnp.broadcast_to(ids, (16, LANES)).astype(BF16)
    copies[3].wait()
    first = core_ref[0] == 0
    for c in range(CHUNKS // 2):
        even = cotangent_ref[:, 2 * c * LANES : (2 * c + 1) * LANES]
        odd = cotangent_ref[:, (2 * c + 1) * LANES : (2 * c + 2) * LANES]
        at = slice(c * LANES, (c + 1) * LANES)
        mine_ref[:, at] = jnp.where(first, even, odd)
        theirs_ref[:, at] = jnp.where(first, odd, even)


def normalize(core, frames, ids, gain, cotangent):
    hbm = pl.BlockSpec(memory_space=pltpu.HBM)
    half = jax.ShapeDtypeStruct((ROWS, WIDTH // 2), BF16)
    operands = (frames, ids, gain, cotangent)
    return pl.pallas_call(
        norm_kernel,
        in_specs=[pl.BlockSpec(memory_space=pltpu.SMEM)] + [hbm] * len(operands),
        out_shape=[jax.ShapeDtypeStruct((PACKED, LANES), BF16), half, half],
        scratch_shapes=[pltpu.VMEM(x.shape, x.dtype) for x in operands]
        + [pltpu.SemaphoreType.DMA((len(operands),))],
        compiler_params=pltpu.CompilerParams(vmem_limit_bytes=60 * 1024 * 1024),
        name="layer_norm",
    )(core, *operands)


def unpacked(block):
    ref, slot = block
    base = slot * PACKED
    chunks = [ref[base + c * ROWS : base + (c + 1) * ROWS, :] for c in range(CHUNKS)]
    return jnp.concatenate(chunks, axis=1)


def id_row(block):
    ref, slot = block
    base = slot * PACKED + WIDTH
    return ref[base : base + 16, :].astype(F32)[0:1, :]


def id_column(row):
    across = lax.broadcasted_iota(jnp.int32, (ROWS, LANES), 1)
    down = lax.broadcasted_iota(jnp.int32, (ROWS, LANES), 0)
    return jnp.sum(jnp.where(across == down, row, 0.0), axis=1, keepdims=True)


def projected(frames, weight_ref, section, quad):
    at = section * WIDTH + quad * QUAD
    block = weight_ref[:, at : at + QUAD]
    return jnp.dot(frames, block, preferred_element_type=F32).astype(BF16)


def absorb(frames, bias, queries_ref, weight_ref, state, first):
    tops_ref, sums_ref, acc_ref = state
    both = jnp.concatenate([bias, bias], axis=1)
    pairs = 2 * QUADS
    keys, flipped, waiting = {}, {}, []

    def score(index):
        quad, at = index // 2, (index % 2) * LANES
        if quad not in keys:
            keys[quad] = projected(frames, weight_ref, 1, quad)
            flipped[quad] = jnp.transpose(projected(frames, weight_ref, 2, quad))
        part = keys[quad][:, at : at + LANES]
        return jnp.dot(part, queries_ref[index], preferred_element_type=F32) + both

    for index in range(pairs + AHEAD):
        if index < pairs:
            waiting.append(score(index))
        if index < AHEAD:
            continue
        pair = index - AHEAD
        heads = (2 * pair, 2 * pair + 1)
        scores = waiting[pair]
        waiting[pair] = None
        top = jnp.max(scores, axis=0, keepdims=True)
        if not first:
            old_top = jnp.concatenate([tops_ref[h : h + 1, :] for h in heads], axis=1)
            old_sum = jnp.concatenate([sums_ref[h : h + 1, :] for h in heads], axis=1)
            top = jnp.maximum(old_top, top)
            rescale = jnp.exp2((old_top - top) * LOG2E)
        weights = jnp.exp2((scores - top) * LOG2E)
        total = jnp.sum(weights, axis=0, keepdims=True)
        at = (pair % 2) * LANES
        values = flipped[pair // 2][at : at + LANES, :]
        mixed = jnp.dot(values, weights.astype(BF16), preferred_element_type=F32)
        if not first:
            total = old_sum * rescale + total
        for k, h in enumerate(heads):
            lanes = slice(k * LANES, (k + 1) * LANES)
            rows = slice(h * HALF, (h + 1) * HALF)
            term = mixed[k * HALF : (k + 1) * HALF, lanes]
            if not first:
                term = acc_ref[rows, :] * rescale[:, lanes] + term
            acc_ref[rows, :] = term
            tops_ref[h : h + 1, :] = top[:, lanes]
            sums_ref[h : h + 1, :] = total[:, lanes]


def bias_of(blocks, own_row):
    columns = jnp.concatenate([id_column(id_row(block)) for block in blocks], axis=0)
    return jnp.where(columns == own_row, 0.0, NEG_BIG)


def own_kernel(own_ref, weight_ref, queries_ref, *state):
    frames = unpacked((own_ref, 0))
    row = id_row((own_ref, 0))
    for quad in range(QUADS):
        queries = projected(frames, weight_ref, 0, quad) * jnp.asarray(0.125, BF16)
        flipped = jnp.transpose(queries)
        zeros = jnp.zeros((HALF, ROWS), BF16)
        for pair in range(2):
            index = 2 * quad + pair
            at = pair * LANES
            queries_ref[index, 0:HALF, 0:ROWS] = flipped[at : at + HALF, :]
            queries_ref[index, 0:HALF, ROWS:] = zeros
            queries_ref[index, HALF:, 0:ROWS] = zeros
            queries_ref[index, HALF:, ROWS:] = flipped[at + HALF : at + LANES, :]
    absorb(frames, bias_of(((own_ref, 0),), row), queries_ref, weight_ref, state, True)


STATE_SHAPES = (
    jax.ShapeDtypeStruct((2 * CHUNKS, LANES), F32),
    jax.ShapeDtypeStruct((2 * CHUNKS, LANES), F32),
    jax.ShapeDtypeStruct((WIDTH, LANES), F32),
)


def cost(blocks, mib):
    return pl.CostEstimate(
        flops=2 * blocks * ROWS * WIDTH * 2 * WIDTH, bytes_accessed=mib << 20, transcendentals=0
    )


def own_block(own, w_qkv):
    return pl.pallas_call(
        own_kernel,
        out_shape=[jax.ShapeDtypeStruct((CHUNKS, LANES, 2 * ROWS), BF16), *STATE_SHAPES],
        compiler_params=LIMIT,
        cost_estimate=cost(3, 8),
        name="own_block",
    )(own, w_qkv)


def absorb_both(own_ref, left, right, queries_ref, weight_ref, state):
    own_row = id_row((own_ref, 0))
    left_needed = jnp.max(id_row(left[0])) == jnp.min(own_row)
    right_needed = jnp.min(id_row(right[0])) == jnp.max(own_row)

    @pl.when(left_needed | right_needed)
    def _():
        blocks = (*left, *right)
        frames = jnp.concatenate([unpacked(block) for block in blocks], axis=0)
        absorb(frames, bias_of(blocks, own_row), queries_ref, weight_ref, state, False)


def located(refs, places):
    return [(refs[i], slot) for i, slot in places]


def copied(old_state, state):
    for old, new in zip(old_state, state):
        new[...] = old[...]


def absorb_stage(own, blocks, left, right, queries, w_qkv, state):
    count = len(blocks)

    def kernel(own_ref, *refs):
        block_refs, refs = refs[:count], refs[count:]
        queries_ref, weight_ref = refs[:2]
        copied(refs[2:5], refs[5:8])
        absorb_both(
            own_ref, located(block_refs, left), located(block_refs, right), queries_ref, weight_ref, refs[5:8]
        )

    return pl.pallas_call(
        kernel,
        out_shape=list(STATE_SHAPES),
        compiler_params=LIMIT,
        cost_estimate=cost(len(left) + len(right), 8),
        name="absorb_stage",
    )(own, *blocks, queries, w_qkv, *state)


def last_stage(own, blocks, left, right, queries, w_qkv, state, frames, w_out):
    count = len(blocks)

    def kernel(own_ref, *refs):
        block_refs, refs = refs[:count], refs[count:]
        queries_ref, weight_ref = refs[:2]
        frames_ref, wout_ref, attended_ref, out_ref = refs[5:9]
        state_refs = refs[9:12]
        copied(refs[2:5], state_refs)
        absorb_both(
            own_ref, located(block_refs, left), located(block_refs, right), queries_ref, weight_ref, state_refs
        )
        _, sums_ref, acc_ref = state_refs
        n_y, rows = attended_ref.shape[0], WIDTH // N_SEQ
        chunks = []
        for c in range(CHUNKS):
            parts = []
            for h in (2 * c, 2 * c + 1):
                parts.append((acc_ref[h * HALF : (h + 1) * HALF, :] / sums_ref[h : h + 1, :]).astype(BF16))
            chunk = jnp.concatenate(parts, axis=0)
            for k in range(LANES // rows):
                z, y = divmod(c * (LANES // rows) + k, n_y)
                attended_ref[y, z * rows : (z + 1) * rows, :] = chunk[k * rows : (k + 1) * rows, :]
            chunks.append(jnp.transpose(chunk))
        attended = jnp.concatenate(chunks, axis=1)
        product = jnp.dot(attended, wout_ref[...], preferred_element_type=F32)
        out_ref[...] = (frames_ref[...].astype(F32) + product).astype(BF16)

    return pl.pallas_call(
        kernel,
        out_shape=[
            jax.ShapeDtypeStruct((N_Y, WIDTH // N_Y, LANES), BF16),
            jax.ShapeDtypeStruct((ROWS, WIDTH), BF16),
        ],
        scratch_shapes=[pltpu.VMEM(shape.shape, F32) for shape in STATE_SHAPES],
        compiler_params=LIMIT,
        cost_estimate=cost(len(left) + len(right) + 1, 10),
        name="last_stage",
    )(own, *blocks, queries, w_qkv, *state, frames, w_out)


def grad_kernel(place_ref, own_ref, other_ref, *refs):
    grads, out_ref = refs[:-1], refs[-1]
    count = len(grads)
    order = [lax.rem(place_ref[0] + count - i, count) for i in range(count)]
    attended = [ref[i] for i in order for ref in (own_ref, other_ref)]
    attended = jnp.concatenate(attended, axis=1)
    for half in range(2):
        at = slice(half * QUAD, (half + 1) * QUAD)
        block = jnp.concatenate([ref[:, at] for ref in grads], axis=0)
        product = jnp.dot(attended, block, preferred_element_type=F32).astype(BF16)
        for k in range(2):
            out_ref[2 * half + k] = product[:, k * LANES : (k + 1) * LANES]


def grad_product(place, own, other, grads):
    vmem = pl.BlockSpec(memory_space=pltpu.VMEM)
    rows, columns = own.shape[1], grads[0].shape[1]
    return pl.pallas_call(
        grad_kernel,
        in_specs=[pl.BlockSpec(memory_space=pltpu.SMEM)] + [vmem] * (2 + len(grads)),
        out_shape=jax.ShapeDtypeStruct((columns // LANES, rows, LANES), BF16),
        compiler_params=LIMIT,
        name="grad_product",
    )(place, own, other, *grads)


def local(frames, segment_ids, norm_gain, w_qkv, w_out, cotangent):
    n_y = lax.axis_size("y")
    frames = frames[0]
    core = lax.axis_index("core").astype(jnp.int32).reshape(1)
    place = lax.axis_index("y").astype(jnp.int32).reshape(1)
    own, mine, theirs = normalize(core, frames, segment_ids, norm_gain[None, :], cotangent[0])

    left1, right1 = shifted(own, 1), shifted(own, -1)
    left4, right4 = shifted(own, 4), shifted(own, -4)
    received = core_swapped(theirs)
    queries, *state = own_block(own, w_qkv)
    left1, right1, queries = lax.optimization_barrier((left1, right1, queries))
    near = jnp.concatenate([left1, right1], axis=0)
    left_two, right_two = shifted(near, 4), shifted(near, -4)
    state = absorb_stage(
        own, (left1, left4, right1, right4), ((0, 0), (1, 0)), ((2, 0), (3, 0)), queries, w_qkv, state
    )
    near1, near2, *state = lax.optimization_barrier((left1, right1, *state))
    left2, right2 = shifted(near1, 1), shifted(near2, -1)
    both = jnp.concatenate([mine, received], axis=0)
    both, left_two, right_two = lax.optimization_barrier((both, left_two, right_two))
    left6, right6 = shifted(left_two[:PACKED], 1), shifted(right_two[PACKED:], -1)
    grads = [both, *[turned(both, d) for d in range(1, n_y)]]
    state = absorb_stage(own, (left2, right2), ((0, 0),), ((1, 0),), queries, w_qkv, state)
    state = absorb_stage(
        own, (left_two, right_two), ((0, 1), (0, 0)), ((1, 0), (1, 1)), queries, w_qkv, state
    )
    attended, block_out = last_stage(
        own, (left6, right6), ((0, 0),), ((1, 0),), queries, w_qkv, state, frames, w_out
    )
    attended, grads = lax.optimization_barrier((attended, grads))

    pieces = lax.all_to_all(attended, "y", 0, 0, tiled=True)
    share = grad_product(place, pieces, core_swapped(pieces), grads)
    parts = lax.all_to_all(share.reshape(-1, WIDTH // N_SEQ, LANES), ("x", "z"), 0, 0, tiled=True)
    grad_scale = (lax.axis_size(("x", "core")) * N_SEQ * ROWS) ** (-0.5)
    return (block_out[None], jnp.sum(parts.astype(F32), axis=0) * grad_scale)


def solution(mesh):
    shape = (mesh.shape["dp"] // N_CORE, N_CORE, N_SEQ // N_Y, N_Y)
    chips = Mesh(mesh.devices.reshape(shape), ("x", "core", "z", "y"))
    groups = ("x", "core")
    placed = (P(groups, SEQ, None), P(groups, SEQ), P(), P(), P(), P(groups, SEQ, None))
    return jax.shard_map(
        local,
        mesh=chips,
        in_specs=placed,
        out_specs=(P(groups, SEQ, None), P(SEQ, groups)),
        check_vma=False,
    )
```

```python
import jax
import jax.numpy as jnp
from jax import lax
from jax.experimental import pallas as pl
from jax.experimental.pallas import tpu as pltpu
from jax.sharding import Mesh, PartitionSpec as P

ROWS = 128
LANES = 128
HALF = 64
WIDTH = 1024
CHUNKS = WIDTH // LANES
PACKED = WIDTH + 16
QUAD = 256
QUADS = WIDTH // QUAD
SEQ = ("z", "y")
NEG_BIG = -1e30
EPSILON = 1e-05
N_SEQ = 32
N_Y = 4
N_CORE = 2
LOG2E = 1.4426950408889634
AHEAD = 2
F32 = jnp.float32
BF16 = jnp.bfloat16
LIMIT = pltpu.CompilerParams(vmem_limit_bytes=24 * 1024 * 1024)


def shifted(block, distance):
    n_seq = lax.axis_size(SEQ)
    route = [(i, (i + distance) % n_seq) for i in range(n_seq)]
    return lax.ppermute(block, SEQ, route)


def core_swapped(block):
    return lax.ppermute(block, "core", [(0, 1), (1, 0)])


def turned(block, distance):
    n = lax.axis_size("y")
    return lax.ppermute(block, "y", [(i, (i + distance) % n) for i in range(n)])


def norm_kernel(core_ref, frames_hbm, ids_hbm, gain_hbm, cotangent_hbm, packed_ref, mine_ref, theirs_ref, *scratch):
    frames_ref, ids_ref, gain_ref, cotangent_ref, sems = scratch
    pairs = zip((frames_hbm, ids_hbm, gain_hbm, cotangent_hbm), scratch)
    copies = [pltpu.make_async_copy(src, dst, sems.at[i]) for i, (src, dst) in enumerate(pairs)]
    for copy in copies:
        copy.start()
    for copy in copies[:3]:
        copy.wait()
    float_frames = frames_ref[...].astype(F32)
    average = jnp.mean(float_frames, axis=-1, keepdims=True)
    centered = float_frames - average
    variance = jnp.mean(centered * centered, axis=-1, keepdims=True)
    normed = (centered * lax.rsqrt(variance + EPSILON) * gain_ref[...]).astype(BF16)
    for c in range(CHUNKS):
        packed_ref[c * ROWS : (c + 1) * ROWS, :] = normed[:, c * LANES : (c + 1) * LANES]
    ids = (ids_ref[...] + 1).astype(F32)
    packed_ref[WIDTH:PACKED, :] = jnp.broadcast_to(ids, (16, LANES)).astype(BF16)
    copies[3].wait()
    first = core_ref[0] == 0
    for c in range(CHUNKS // 2):
        even = cotangent_ref[:, 2 * c * LANES : (2 * c + 1) * LANES]
        odd = cotangent_ref[:, (2 * c + 1) * LANES : (2 * c + 2) * LANES]
        at = slice(c * LANES, (c + 1) * LANES)
        mine_ref[:, at] = jnp.where(first, even, odd)
        theirs_ref[:, at] = jnp.where(first, odd, even)


def normalize(core, frames, ids, gain, cotangent):
    hbm = pl.BlockSpec(memory_space=pltpu.HBM)
    half = jax.ShapeDtypeStruct((ROWS, WIDTH // 2), BF16)
    operands = (frames, ids, gain, cotangent)
    return pl.pallas_call(
        norm_kernel,
        in_specs=[pl.BlockSpec(memory_space=pltpu.SMEM)] + [hbm] * len(operands),
        out_shape=[jax.ShapeDtypeStruct((PACKED, LANES), BF16), half, half],
        scratch_shapes=[pltpu.VMEM(x.shape, x.dtype) for x in operands]
        + [pltpu.SemaphoreType.DMA((len(operands),))],
        compiler_params=pltpu.CompilerParams(vmem_limit_bytes=60 * 1024 * 1024),
        name="layer_norm",
    )(core, *operands)


def unpacked(block):
    ref, slot = block
    base = slot * PACKED
    chunks = [ref[base + c * ROWS : base + (c + 1) * ROWS, :] for c in range(CHUNKS)]
    return jnp.concatenate(chunks, axis=1)


def id_row(block):
    ref, slot = block
    base = slot * PACKED + WIDTH
    return ref[base : base + 16, :].astype(F32)[0:1, :]


def id_column(row):
    across = lax.broadcasted_iota(jnp.int32, (ROWS, LANES), 1)
    down = lax.broadcasted_iota(jnp.int32, (ROWS, LANES), 0)
    return jnp.sum(jnp.where(across == down, row, 0.0), axis=1, keepdims=True)


def projected(frames, weight_ref, section, quad):
    at = section * WIDTH + quad * QUAD
    block = weight_ref[:, at : at + QUAD]
    return jnp.dot(frames, block, preferred_element_type=F32).astype(BF16)


def absorb(frames, bias, queries_ref, weight_ref, state, first):
    tops_ref, sums_ref, acc_ref = state
    both = jnp.concatenate([bias, bias], axis=1)
    pairs = 2 * QUADS
    keys, flipped, waiting = {}, {}, []

    def score(index):
        quad, at = index // 2, (index % 2) * LANES
        if quad not in keys:
            keys[quad] = projected(frames, weight_ref, 1, quad)
            flipped[quad] = jnp.transpose(projected(frames, weight_ref, 2, quad))
        part = keys[quad][:, at : at + LANES]
        return jnp.dot(part, queries_ref[index], preferred_element_type=F32) + both

    for index in range(pairs + AHEAD):
        if index < pairs:
            waiting.append(score(index))
        if index < AHEAD:
            continue
        pair = index - AHEAD
        heads = (2 * pair, 2 * pair + 1)
        scores = waiting[pair]
        waiting[pair] = None
        top = jnp.max(scores, axis=0, keepdims=True)
        if not first:
            old_top = jnp.concatenate([tops_ref[h : h + 1, :] for h in heads], axis=1)
            old_sum = jnp.concatenate([sums_ref[h : h + 1, :] for h in heads], axis=1)
            top = jnp.maximum(old_top, top)
            rescale = jnp.exp2((old_top - top) * LOG2E)
        weights = jnp.exp2((scores - top) * LOG2E)
        total = jnp.sum(weights, axis=0, keepdims=True)
        at = (pair % 2) * LANES
        values = flipped[pair // 2][at : at + LANES, :]
        mixed = jnp.dot(values, weights.astype(BF16), preferred_element_type=F32)
        if not first:
            total = old_sum * rescale + total
        for k, h in enumerate(heads):
            lanes = slice(k * LANES, (k + 1) * LANES)
            rows = slice(h * HALF, (h + 1) * HALF)
            term = mixed[k * HALF : (k + 1) * HALF, lanes]
            if not first:
                term = acc_ref[rows, :] * rescale[:, lanes] + term
            acc_ref[rows, :] = term
            tops_ref[h : h + 1, :] = top[:, lanes]
            sums_ref[h : h + 1, :] = total[:, lanes]


def bias_of(blocks, own_row):
    columns = jnp.concatenate([id_column(id_row(block)) for block in blocks], axis=0)
    return jnp.where(columns == own_row, 0.0, NEG_BIG)


def own_kernel(own_ref, weight_ref, queries_ref, *state):
    frames = unpacked((own_ref, 0))
    row = id_row((own_ref, 0))
    for quad in range(QUADS):
        queries = projected(frames, weight_ref, 0, quad) * jnp.asarray(0.125, BF16)
        flipped = jnp.transpose(queries)
        zeros = jnp.zeros((HALF, ROWS), BF16)
        for pair in range(2):
            index = 2 * quad + pair
            at = pair * LANES
            queries_ref[index, 0:HALF, 0:ROWS] = flipped[at : at + HALF, :]
            queries_ref[index, 0:HALF, ROWS:] = zeros
            queries_ref[index, HALF:, 0:ROWS] = zeros
            queries_ref[index, HALF:, ROWS:] = flipped[at + HALF : at + LANES, :]
    absorb(frames, bias_of(((own_ref, 0),), row), queries_ref, weight_ref, state, True)


STATE_SHAPES = (
    jax.ShapeDtypeStruct((2 * CHUNKS, LANES), F32),
    jax.ShapeDtypeStruct((2 * CHUNKS, LANES), F32),
    jax.ShapeDtypeStruct((WIDTH, LANES), F32),
)


def cost(blocks, mib):
    return pl.CostEstimate(
        flops=2 * blocks * ROWS * WIDTH * 2 * WIDTH, bytes_accessed=mib << 20, transcendentals=0
    )


def own_block(own, w_qkv):
    return pl.pallas_call(
        own_kernel,
        out_shape=[jax.ShapeDtypeStruct((CHUNKS, LANES, 2 * ROWS), BF16), *STATE_SHAPES],
        compiler_params=LIMIT,
        cost_estimate=cost(3, 8),
        name="own_block",
    )(own, w_qkv)


def absorb_both(own_ref, left, right, queries_ref, weight_ref, state):
    own_row = id_row((own_ref, 0))
    left_needed = jnp.max(id_row(left[0])) == jnp.min(own_row)
    right_needed = jnp.min(id_row(right[0])) == jnp.max(own_row)

    @pl.when(left_needed | right_needed)
    def _():
        blocks = (*left, *right)
        frames = jnp.concatenate([unpacked(block) for block in blocks], axis=0)
        absorb(frames, bias_of(blocks, own_row), queries_ref, weight_ref, state, False)


def located(refs, places):
    return [(refs[i], slot) for i, slot in places]


def copied(old_state, state):
    for old, new in zip(old_state, state):
        new[...] = old[...]


def absorb_stage(own, blocks, left, right, queries, w_qkv, state):
    count = len(blocks)

    def kernel(own_ref, *refs):
        block_refs, refs = refs[:count], refs[count:]
        queries_ref, weight_ref = refs[:2]
        copied(refs[2:5], refs[5:8])
        absorb_both(
            own_ref, located(block_refs, left), located(block_refs, right), queries_ref, weight_ref, refs[5:8]
        )

    return pl.pallas_call(
        kernel,
        out_shape=list(STATE_SHAPES),
        compiler_params=LIMIT,
        cost_estimate=cost(len(left) + len(right), 8),
        name="absorb_stage",
    )(own, *blocks, queries, w_qkv, *state)


def last_stage(own, blocks, left, right, queries, w_qkv, state):
    count = len(blocks)

    def kernel(own_ref, *refs):
        block_refs, refs = refs[:count], refs[count:]
        queries_ref, weight_ref = refs[:2]
        attended_ref, natural_ref = refs[5:7]
        state_refs = refs[7:10]
        copied(refs[2:5], state_refs)
        absorb_both(
            own_ref, located(block_refs, left), located(block_refs, right), queries_ref, weight_ref, state_refs
        )
        _, sums_ref, acc_ref = state_refs
        n_y, rows = attended_ref.shape[0], WIDTH // N_SEQ
        for c in range(CHUNKS):
            parts = []
            for h in (2 * c, 2 * c + 1):
                parts.append((acc_ref[h * HALF : (h + 1) * HALF, :] / sums_ref[h : h + 1, :]).astype(BF16))
            chunk = jnp.concatenate(parts, axis=0)
            for k in range(LANES // rows):
                z, y = divmod(c * (LANES // rows) + k, n_y)
                attended_ref[y, z * rows : (z + 1) * rows, :] = chunk[k * rows : (k + 1) * rows, :]
            natural_ref[:, c * LANES : (c + 1) * LANES] = jnp.transpose(chunk)

    return pl.pallas_call(
        kernel,
        out_shape=[
            jax.ShapeDtypeStruct((N_Y, WIDTH // N_Y, LANES), BF16),
            jax.ShapeDtypeStruct((ROWS, WIDTH), BF16),
        ],
        scratch_shapes=[pltpu.VMEM(shape.shape, F32) for shape in STATE_SHAPES],
        compiler_params=LIMIT,
        cost_estimate=cost(len(left) + len(right) + 1, 10),
        name="last_stage",
    )(own, *blocks, queries, w_qkv, *state)


def project_kernel(attended_ref, wout_ref, frames_ref, out_ref):
    product = jnp.dot(attended_ref[...], wout_ref[...], preferred_element_type=F32)
    out_ref[...] = (frames_ref[...].astype(F32) + product).astype(BF16)


def project(attended, w_out, frames):
    return pl.pallas_call(
        project_kernel,
        out_shape=jax.ShapeDtypeStruct((ROWS, WIDTH), BF16),
        compiler_params=LIMIT,
        cost_estimate=pl.CostEstimate(
            flops=2 * ROWS * WIDTH * WIDTH, bytes_accessed=3 << 20, transcendentals=0
        ),
        name="project",
    )(attended, w_out, frames)


def grad_kernel(place_ref, own_ref, other_ref, *refs):
    grads, out_ref = refs[:-1], refs[-1]
    count = len(grads)
    order = [lax.rem(place_ref[0] + count - i, count) for i in range(count)]
    attended = [ref[i] for i in order for ref in (own_ref, other_ref)]
    attended = jnp.concatenate(attended, axis=1)
    for half in range(2):
        at = slice(half * QUAD, (half + 1) * QUAD)
        block = jnp.concatenate([ref[:, at] for ref in grads], axis=0)
        product = jnp.dot(attended, block, preferred_element_type=F32).astype(BF16)
        for k in range(2):
            out_ref[2 * half + k] = product[:, k * LANES : (k + 1) * LANES]


def grad_product(place, own, other, grads):
    vmem = pl.BlockSpec(memory_space=pltpu.VMEM)
    rows, columns = own.shape[1], grads[0].shape[1]
    return pl.pallas_call(
        grad_kernel,
        in_specs=[pl.BlockSpec(memory_space=pltpu.SMEM)] + [vmem] * (2 + len(grads)),
        out_shape=jax.ShapeDtypeStruct((columns // LANES, rows, LANES), BF16),
        compiler_params=LIMIT,
        name="grad_product",
    )(place, own, other, *grads)


def local(frames, segment_ids, norm_gain, w_qkv, w_out, cotangent):
    n_y = lax.axis_size("y")
    frames = frames[0]
    core = lax.axis_index("core").astype(jnp.int32).reshape(1)
    place = lax.axis_index("y").astype(jnp.int32).reshape(1)
    own, mine, theirs = normalize(core, frames, segment_ids, norm_gain[None, :], cotangent[0])

    left1, right1 = shifted(own, 1), shifted(own, -1)
    left4, right4 = shifted(own, 4), shifted(own, -4)
    received = core_swapped(theirs)
    queries, *state = own_block(own, w_qkv)
    left1, right1, queries = lax.optimization_barrier((left1, right1, queries))
    near = jnp.concatenate([left1, right1], axis=0)
    left_two, right_two = shifted(near, 4), shifted(near, -4)
    state = absorb_stage(
        own, (left1, left4, right1, right4), ((0, 0), (1, 0)), ((2, 0), (3, 0)), queries, w_qkv, state
    )
    near1, near2, *state = lax.optimization_barrier((left1, right1, *state))
    left2, right2 = shifted(near1, 1), shifted(near2, -1)
    both = jnp.concatenate([mine, received], axis=0)
    both, left_two, right_two = lax.optimization_barrier((both, left_two, right_two))
    left6, right6 = shifted(left_two[:PACKED], 1), shifted(right_two[PACKED:], -1)
    grads = [both, *[turned(both, d) for d in range(1, n_y)]]
    state = absorb_stage(own, (left2, right2), ((0, 0),), ((1, 0),), queries, w_qkv, state)
    state = absorb_stage(
        own, (left_two, right_two), ((0, 1), (0, 0)), ((1, 0), (1, 1)), queries, w_qkv, state
    )
    attended, natural = last_stage(own, (left6, right6), ((0, 0),), ((1, 0),), queries, w_qkv, state)
    attended, grads = lax.optimization_barrier((attended, grads))

    block_out = project(natural, w_out, frames)
    pieces = lax.all_to_all(attended, "y", 0, 0, tiled=True)
    share = grad_product(place, pieces, core_swapped(pieces), grads)
    parts = lax.all_to_all(share.reshape(-1, WIDTH // N_SEQ, LANES), ("x", "z"), 0, 0, tiled=True)
    grad_scale = (lax.axis_size(("x", "core")) * N_SEQ * ROWS) ** (-0.5)
    return (block_out[None], jnp.sum(parts.astype(F32), axis=0) * grad_scale)


def solution(mesh):
    shape = (mesh.shape["dp"] // N_CORE, N_CORE, N_SEQ // N_Y, N_Y)
    chips = Mesh(mesh.devices.reshape(shape), ("x", "core", "z", "y"))
    groups = ("x", "core")
    placed = (P(groups, SEQ, None), P(groups, SEQ), P(), P(), P(), P(groups, SEQ, None))
    return jax.shard_map(
        local,
        mesh=chips,
        in_specs=placed,
        out_specs=(P(groups, SEQ, None), P(SEQ, groups)),
        check_vma=False,
    )
```
